256 devices in a mesh: replica: 8 (over x, core), tensor: 32 (over y, z).
Axes of the slice: x: 4, y: 4, z: 8, core: 2. Of those that a mesh axis runs over, the one named last changes fastest.
Arguments:
- kv_pool: bfloat16 [8, 512, 32, 2048], P('replica', 'tensor'), may hold values from -6 to 6
- page_table: int32 [8, 4, 128], P('replica', None, 'tensor'), may hold values from 0 to 15, as said below
- lengths: int32 [8, 4], replicated, may hold values from 1 to 4096, as said below
- steal_plan: int32 [8, 3, 2], replicated, may hold values from 0 to 7, as said below
- hidden_rows: bfloat16 [8, 2, 7, 16384], P('replica', None, None, 'tensor'), may hold values from -6 to 6
- kv_weight: bfloat16 [16384, 2048], P('tensor'), may hold values from -0.046875 to 0.046875
- queries: bfloat16 [8, 2, 7, 16384], P('replica', None, None, 'tensor'), may hold values from -300 to 300
Outputs:
- attended: bfloat16 [8, 2, 7, 16384], P('replica', None, None, 'tensor')
The draws below stay inside these ranges and needn't reach their ends.
Inputs may be any that keep to these rules, and one draw needn't show every extreme that they name: `page_table`: on each tensor device t, columns t * 4 to t * 4 + 3 of all 4 requests of a replica name each of its 16 slots once. `lengths`: every replica holds a request of exactly 4096 tokens. `steal_plan`: in row d the source replica is never d; each source named in a row is named exactly 1 times, in consecutive entries.
All inputs are finite; a program needn't handle non-finite values. Where the reference program divides by a largest or mean magnitude, that divisor is 1e-20 or more.
Results may differ from the reference program's by a relative error of at most 0.039.
Values may be sent and summed in bfloat16 or wider, within the bound.
A program may use at most 128 MiB of HBM per device.

```python
import math
import jax
import jax.numpy as jnp
from jax import lax

D = 16384
QH = 128
KVH = 8
HD = 128
ROWS = 4
PAGE = 32
PPD = 4
CAP = 1
STEAL_IN = 3
ROWS_ALL = 7
SLOTS = 16
N_REPLICA = 8
N_TENSOR = 32


def draw_page_table(key, part):
    key = jax.random.fold_in(key, 11)
    keys = jax.random.split(key, N_REPLICA * N_TENSOR)
    orders = jax.vmap(lambda single: jax.random.permutation(single, ROWS * PPD))(keys)
    orders = orders.reshape(N_REPLICA, N_TENSOR, ROWS, PPD).transpose(0, 2, 1, 3)
    return orders.reshape(N_REPLICA, ROWS, N_TENSOR * PPD).astype(jnp.int32)


def draw_lengths(key, part):
    key = jax.random.fold_in(key, 12)
    first, second = jax.random.split(key)
    longest_len = PPD * PAGE * N_TENSOR
    base = jax.random.randint(first, (N_REPLICA, ROWS), 1, longest_len + 1)
    chosen = jax.random.randint(second, (N_REPLICA,), 0, ROWS)
    marked = jnp.arange(ROWS)[None, :] == chosen[:, None]
    return jnp.where(marked, longest_len, base).astype(jnp.int32)


def draw_steal_plan(key, part):
    key = jax.random.fold_in(key, 13)
    first, second = jax.random.split(key)
    keys = jax.random.split(first, N_REPLICA)
    offsets = jax.vmap(lambda single: jax.random.permutation(single, N_REPLICA - 1))(keys)
    offsets = jnp.repeat(offsets[:, :STEAL_IN // CAP] + 1, CAP, axis=1)
    source = (jnp.arange(N_REPLICA)[:, None] + offsets) % N_REPLICA
    taken = jax.random.randint(second, (N_REPLICA, STEAL_IN), 0, ROWS)
    return jnp.stack([source, taken], axis=-1).astype(jnp.int32)


def draw_queries(key, part):
    key = jax.random.fold_in(key, 14)
    first = jax.random.fold_in(key, 0)
    shape = (N_REPLICA, 2, ROWS_ALL, QH * HD)
    values = jnp.clip(jax.random.normal(first, shape, jnp.float32), -6.0, 6.0)
    return values.astype(jnp.bfloat16)


def levels(rng, dims, cuts, low, largest):
    def one(position, parts):
        heights = jax.random.uniform(jax.random.fold_in(jax.random.fold_in(rng, 6), position), (parts,), jnp.float32, low / len(cuts), largest / len(cuts))
        return jnp.repeat(jnp.exp(heights), dims[position] // parts).reshape((-1,) + (1,) * (len(dims) - position - 1))

    level = one(*cuts[0])
    for cut in cuts[1:]:
        level = level * one(*cut)
    return level


def centred(rng, shape, scale, bound, cuts=(), kind=jnp.bfloat16):
    result = jax.random.normal(rng, shape, jnp.float32) * scale
    if len(cuts) > 0:
        result = levels(rng, shape, cuts, -0.22, 0.18) * result
    return jnp.clip(result, min=-bound, max=bound).astype(kind)


def setup_inputs(seed: int = 0) -> dict:
    splits = jax.random.split(jax.random.key(seed), 8)
    kv_pool = centred(splits[0], (N_REPLICA, N_TENSOR * SLOTS, PAGE, 2 * KVH * HD), 1.0, 6.0, ((0, 8), (1, 32)))
    page_table = draw_page_table(jax.random.fold_in(splits[7], 71), 0)
    lengths = draw_lengths(jax.random.fold_in(splits[7], 71), 0)
    steal_plan = draw_steal_plan(jax.random.fold_in(splits[7], 71), 0)
    hidden_rows = centred(splits[4], (N_REPLICA, 2, ROWS_ALL, D), 1.0, 6.0, ((0, 8), (3, 32)))
    kv_weight = centred(splits[5], (D, 2 * KVH * HD), D ** -0.5, 0.046875, ((0, 32),))
    queries = draw_queries(jax.random.fold_in(splits[7], 71), 0)
    return dict(kv_pool=kv_pool, page_table=page_table, lengths=lengths, steal_plan=steal_plan, hidden_rows=hidden_rows, kv_weight=kv_weight, queries=queries)


masked_score = -1e+30

def hadamard(order):
    counter = jnp.arange(order, dtype=jnp.int32)
    intersection = jnp.bitwise_and(counter[:, None], counter[None, :])
    parity = jnp.zeros((order, order), jnp.int32)
    for bit_index in range(order.bit_length() - 1):
        parity = parity + jnp.bitwise_and(jnp.right_shift(intersection, bit_index), 1)
    signs = 1.0 - 2.0 * jnp.bitwise_and(parity, 1).astype(jnp.float32)
    return signs / math.sqrt(order)

def rotate_pack(leaving, rotation):
    shaped = leaving.astype(jnp.float32).reshape(leaving.shape[:-1] + (2 * KVH, HD))
    turned = jnp.einsum('...d,de->...e', shaped, rotation, precision=lax.Precision.HIGHEST)
    scales = lax.optimization_barrier((lax.optimization_barrier(jnp.max(jnp.abs(turned), axis=-1)) + 1e-06).astype(jnp.bfloat16))
    packed = (turned / scales.astype(jnp.float32)[..., None]).astype(jnp.bfloat16)
    return (packed.reshape(leaving.shape), scales)

def unpack(packed, scales, rotation):
    packed = lax.optimization_barrier(packed)
    shaped = packed.astype(jnp.float32).reshape(packed.shape[:-1] + (2 * KVH, HD))
    shaped = shaped * scales.astype(jnp.float32)[..., None]
    back = jnp.einsum('...d,de->...e', shaped, rotation, precision=lax.Precision.HIGHEST)
    return back.reshape(packed.shape).astype(jnp.bfloat16)

def attend(query_rows, keys, fresh, spans, key_position):
    keys = lax.optimization_barrier(keys)
    rows_all = keys.shape[0]
    group = QH // KVH
    query = query_rows.astype(jnp.float32).reshape(2, rows_all, KVH, group, HD)
    key_part = keys[..., :KVH * HD].astype(jnp.float32).reshape(rows_all, -1, KVH, HD)
    value_part = keys[..., KVH * HD:].astype(jnp.float32).reshape(rows_all, -1, KVH, HD)
    new_keys = fresh[..., :KVH * HD].astype(jnp.float32).reshape(2, rows_all, KVH, HD)
    new_values = fresh[..., KVH * HD:].astype(jnp.float32).reshape(2, rows_all, KVH, HD)
    factor = 1.0 / math.sqrt(HD)
    score = jnp.einsum('srkgd,rlkd->srkgl', query, key_part) * factor
    valid = key_position[None, :] < spans[:, None]
    score = jnp.where(valid[None, :, None, None, :], score, masked_score)
    tail = jnp.einsum('srkgd,trkd->srkgt', query, new_keys) * factor
    step_index = jnp.arange(2, dtype=jnp.int32)
    tail_mask = step_index[None, :] <= step_index[:, None]
    tail = jnp.where(tail_mask[:, None, None, None, :], tail, masked_score)
    top = jnp.maximum(lax.optimization_barrier(jnp.max(score, axis=-1)), lax.optimization_barrier(jnp.max(tail, axis=-1)))
    weights = jnp.exp(score - top[..., None])
    tail_weights = jnp.exp(tail - top[..., None])
    total = lax.optimization_barrier(jnp.sum(weights, axis=-1)) + lax.optimization_barrier(jnp.sum(tail_weights, axis=-1))
    light = lax.optimization_barrier(weights.astype(jnp.bfloat16)).astype(jnp.float32)
    tail_light = lax.optimization_barrier(tail_weights.astype(jnp.bfloat16)).astype(jnp.float32)
    mixed = jnp.einsum('srkgl,rlkd->srkgd', light, value_part)
    mixed = mixed + jnp.einsum('srkgt,trkd->srkgd', tail_light, new_values)
    return (mixed / total[..., None]).reshape(2, rows_all, QH * HD).astype(jnp.bfloat16)

def reference(kv_pool, page_table, lengths, steal_plan, hidden_rows, kv_weight, queries):
    rotation = hadamard(HD)
    width = 2 * KVH * HD
    fresh = jnp.dot(hidden_rows.reshape(-1, D), kv_weight, preferred_element_type=jnp.float32)
    fresh = fresh.astype(jnp.bfloat16).reshape(N_REPLICA, 2, ROWS_ALL, width)
    column = jnp.arange(N_TENSOR * PPD, dtype=jnp.int32)
    device_of = column // PPD
    page_of = column % PPD
    slot_base = device_of * SLOTS
    page_start = (page_of * N_TENSOR + device_of) * PAGE
    key_position = (page_start[:, None] + jnp.arange(PAGE, dtype=jnp.int32)[None, :]).reshape(-1)

    def pages_of(group, request):
        where = page_table[group, request] + slot_base
        return kv_pool[group, where].reshape(-1, width)

    def one_replica(dest):
        own = jax.vmap(lambda request: pages_of(dest, request))(jnp.arange(ROWS, dtype=jnp.int32))
        sources = steal_plan[dest, :, 0]
        requested = steal_plan[dest, :, 1]
        moved = jax.vmap(pages_of)(sources, requested)
        packed, scales = rotate_pack(moved, rotation)
        moved = unpack(packed, scales, rotation)
        keys = jnp.concatenate([own, moved], axis=0)
        spans = jnp.concatenate([lengths[dest], lengths[sources, requested]])
        return attend(queries[dest], keys, fresh[dest], spans, key_position)
    return lax.map(one_replica, jnp.arange(N_REPLICA, dtype=jnp.int32))
```

```python
import functools
import math

import jax
import jax.numpy as jnp
from jax import lax
from jax.experimental import pallas as pl
from jax.experimental.pallas import tpu as pltpu
from jax.sharding import PartitionSpec as P

KVH = 8
HD = 128
PAGE = 32
PPD = 4
STEAL_IN = 3
ROWS = 4
ROWS_ALL = 7
SLOTS = 16
NR = 8
NY = 4
NZ = 8
NT = NY * NZ
MASKED = -1e30
MESH = pl.DeviceIdType.MESH
F32 = jnp.float32
BF16 = jnp.bfloat16
INV = 1.0 / math.sqrt(HD)
NPO = 2
NPS = 4


def lanes(shape):
    return lax.broadcasted_iota(jnp.int32, shape, len(shape) - 1)


def rolled(x, by):
    return pltpu.roll(x, by % 128, 1)


def halves(x):
    high = x.astype(BF16).astype(F32)
    return high, (x - high).astype(BF16).astype(F32)


def merged_stats(tiles, pairs):
    tops, totals = [], []
    for tile in tiles:
        both = tile + rolled(tile, -pairs)
        tops.append(both)
        totals.append(rolled(both, -2 * pairs))
    top = functools.reduce(jnp.maximum, tops)
    factors = [jnp.exp(one - top) for one in tops]
    total = sum(f * l for f, l in zip(factors, totals))
    return top, total, factors


def kernel(
    table, lengths, plan, q_ref, h_ref, pool_hbm, w_hbm, out_ref,
    pool, moved, w, qt, qo, qs, xsend, xrecv, fsend, frecv, fsum, fz, fresh,
    obo, obs, rbo, rbs, sto, sts, mbo, mbs, zbo, zbs, bsend, brecv, fin,
    lsem, ss, rs,
):
    me = lax.axis_index("replica")
    t = lax.axis_index("tensor")
    y, z = t // NZ, t % NZ
    ypeer = [None] + [(me, ((y + o) % NY) * NZ + z) for o in range(1, NY)]
    zpeer = [None] + [(me, y * NZ + (z + o) % NZ) for o in range(1, NZ)]
    xpeer = [None] + [((me + o) % NR, t) for o in range(1, NR)]
    zorder = (1, 7, 2, 6, 3, 5, 4)

    pool_copy = pltpu.make_async_copy(pool_hbm, pool, lsem.at[0])
    w_copy = pltpu.make_async_copy(w_hbm, w, lsem.at[1])
    w_copy.start()
    pool_copy.start()

    barrier = pltpu.get_barrier_semaphore()
    peers = zpeer[1:] + ypeer[1:] + xpeer[1:]
    for peer in peers:
        pl.semaphore_signal(barrier, inc=1, device_id=peer, device_id_type=MESH)

    for s in range(2):
        for j in range(4):
            qt[pl.ds(s * 4 + j, ROWS_ALL, stride=8), :] = q_ref[s, :, j * HD:(j + 1) * HD].astype(F32)
    qo[t] = qt[0:32].astype(BF16)
    for o in range(1, NR):
        source = (me + o) % NR
        chosen = jnp.zeros((8, HD), F32)
        for e in range(STEAL_IN):
            tile = qt[(ROWS + e) * 8:(ROWS + e + 1) * 8]
            chosen = chosen + jnp.where(plan[me, e, 0] == source, tile, 0.0)
        xsend[o] = chosen
    xrecv[me] = jnp.zeros((8, HD), F32)
    sto[...] = jnp.zeros_like(sto)
    sts[...] = jnp.zeros_like(sts)

    count = [0, 0]
    sends = []

    def fresh_index(kind, n=1):
        first = count[kind]
        count[kind] += n
        return first

    def push(src, dst, recv, peer):
        copy = pltpu.make_async_remote_copy(
            src_ref=src, dst_ref=dst, send_sem=ss.at[fresh_index(0)], recv_sem=rs.at[recv],
            device_id=peer, device_id_type=MESH,
        )
        copy.start()
        sends.append(copy)

    def arrive(dst, recv):
        pltpu.make_async_remote_copy(
            src_ref=dst, dst_ref=dst, send_sem=ss.at[0], recv_sem=rs.at[recv],
            device_id=xpeer[1], device_id_type=MESH,
        ).wait_recv()

    x_r = fresh_index(1, NR)
    qoz_r = fresh_index(1, NZ)
    qoy_r = fresh_index(1, NY)
    qsz_r = fresh_index(1, NZ)
    qsy_r = fresh_index(1, NY)
    fy_r = fresh_index(1, NY)
    fz_r = fresh_index(1, NZ)
    oy_r = fresh_index(1, NY)
    sy_r = fresh_index(1, NY)
    oz_r = fresh_index(1, NZ)
    sz_r = fresh_index(1, NZ)
    b_r = fresh_index(1, NR)

    pl.semaphore_wait(barrier, len(peers))

    for o in range(1, NR):
        push(xsend.at[o], xrecv.at[me], x_r + o, xpeer[o])
    for o in zorder:
        push(qo.at[t], qo.at[t], qoz_r + o, zpeer[o])
    for o in range(1, NY):
        push(qo.at[t], qo.at[t], qoy_r + o, ypeer[o])

    w_copy.wait()
    hidden = jnp.concatenate(
        [h_ref[0].astype(F32), jnp.zeros((1, 512), F32), h_ref[1].astype(F32), jnp.zeros((1, 512), F32)], axis=0
    ).astype(BF16)
    for kind in range(2):
        for k in range(0, KVH, 2):
            first = (kind * KVH + k) * HD
            part = jnp.dot(hidden, w[:, first:first + 2 * HD], preferred_element_type=F32)
            fsend[k // 2, 0, kind] = part[:, :HD]
            fsend[k // 2, 1, kind] = part[:, HD:]

    def forward(buf, chunk_r, out_r, offsets):
        for o in offsets:
            at = y * NZ + (z - o) % NZ
            arrive(buf.at[at], chunk_r + o)
            for yo in range(1, NY):
                push(buf.at[at], buf.at[at], out_r + yo, ypeer[yo])

    forward(qo, qoz_r, qoy_r, (1, 7))
    for o in range(1, NR):
        arrive(xrecv.at[(me - o) % NR], x_r + o)
    qs[t] = xrecv[...].reshape(NR * 8, HD).astype(BF16)
    for o in zorder:
        push(qs.at[t], qs.at[t], qsz_r + o, zpeer[o])
    forward(qo, qoz_r, qoy_r, (2, 6, 3, 5, 4))
    for yo in range(1, NY):
        push(qs.at[t], qs.at[t], qsy_r + yo, ypeer[yo])

    row_id = lax.broadcasted_iota(jnp.int32, (HD, HD), 0)
    both = jnp.bitwise_and(row_id, lanes((HD, HD)))
    parity = jnp.zeros((HD, HD), jnp.int32)
    for bit in range(7):
        parity = parity + jnp.bitwise_and(jnp.right_shift(both, bit), 1)
    signs = (1.0 - 2.0 * jnp.bitwise_and(parity, 1).astype(F32)).astype(BF16)

    pool_copy.wait()

    def round_trip(slot, carry):
        page = pool[slot]
        rows = jnp.concatenate([page[:, i * HD:(i + 1) * HD] for i in range(2 * KVH)], axis=0)
        turned = jnp.dot(rows, signs, preferred_element_type=F32) * INV
        scales = (jnp.max(jnp.abs(turned), axis=1, keepdims=True) + 1e-06).astype(BF16).astype(F32)
        packed = (turned * (1.0 / scales)).astype(BF16)
        back = (jnp.dot(packed, signs, preferred_element_type=F32) * (scales * INV)).astype(BF16)
        for i in range(2 * KVH):
            moved[slot, :, i * HD:(i + 1) * HD] = back[i * PAGE:(i + 1) * PAGE]
        return carry

    lax.fori_loop(0, SLOTS // 2, round_trip, 0)
    forward(qs, qsz_r, qsy_r, (1, 7, 2, 6, 3, 5, 4))
    for yo in range(1, NY):
        push(fsend.at[(y + yo) % NY], frecv.at[yo - 1], fy_r + yo, ypeer[yo])
    lax.fori_loop(SLOTS // 2, SLOTS, round_trip, 0)

    row16 = lax.broadcasted_iota(jnp.int32, (64, HD), 0) % 16
    lane64 = lanes((64, HD))
    first_half = row16 < 8
    mask_a = jnp.where(first_half, 1.0, 0.0).astype(BF16)
    mask_b = jnp.where(first_half, 0.0, 1.0).astype(BF16)
    place = ((lane64 // PAGE) * NT + t) * PAGE + lane64 % PAGE
    dest = lax.broadcasted_iota(jnp.int32, (64, HD), 0) // 16

    def attend(pages, queries, results, stats, pairs, describe, p):
        (slots_a, span_a), (slots_b, span_b) = describe(2 * p), describe(2 * p + 1)
        valid = place < jnp.where(first_half, span_a, span_b)
        at = pl.multiple_of(p * 16, 16)

        def tokens(slots, first):
            return jnp.concatenate([pages[slot, :, first:first + HD] for slot in slots], axis=0)

        for k in range(KVH):
            query = queries[4 * k:4 * k + 4, pl.ds(at, 16), :].reshape(64, HD)
            wide = jnp.concatenate([query * mask_a, query * mask_b], axis=1)
            keys = jnp.concatenate([tokens(slots_a, k * HD), tokens(slots_b, k * HD)], axis=1)
            score = lax.dot_general(wide, keys, (((1,), (1,)), ((), ())), preferred_element_type=F32) * INV
            score = jnp.where(valid, score, MASKED)
            top_high, top_mid = halves(jnp.max(score, axis=1, keepdims=True))
            weights = jnp.where(valid, jnp.exp(score - (top_high + top_mid)), 0.0)
            total_high, total_mid = halves(jnp.sum(weights, axis=1, keepdims=True))
            light = weights.astype(BF16)
            wide = jnp.concatenate([light * mask_a, light * mask_b], axis=1)
            values = jnp.concatenate(
                [tokens(slots_a, (KVH + k) * HD), tokens(slots_b, (KVH + k) * HD)], axis=0
            )
            mixed = jnp.dot(wide, values, preferred_element_type=F32).astype(BF16)
            for j in range(4):
                where = pl.multiple_of(((4 * (k % 2) + j) * pairs + p) * 16, 16)
                results[k // 2, pl.ds(where, 16), :] = mixed[j * 16:(j + 1) * 16]
            lane = lane64 - (4 * (k % 2) + dest) * (4 * pairs) - p
            tile = jnp.where(lane == 0, top_high, 0.0)
            tile = jnp.where(lane == pairs, top_mid, tile)
            tile = jnp.where(lane == 2 * pairs, total_high, tile)
            tile = jnp.where(lane == 3 * pairs, total_mid, tile)
            stats[k // 2] = stats[k // 2] + jnp.sum(tile.reshape(4, 16, HD), axis=0)

    def own(r):
        return [table[r, j] for j in range(PPD)], lengths[me, r]

    def taken(d):
        request = jnp.int32(0)
        for e in range(STEAL_IN):
            request = request + jnp.where(plan[d, e, 0] == me, plan[d, e, 1], 0)
        return [table[request, j] for j in range(PPD)], lengths[me, request]

    def own_pair(p, carry):
        attend(pool, qo, obo, sto, NPO, own, p)
        return carry

    def taken_pair(p, carry):
        attend(moved, qs, obs, sts, NPS, taken, p)
        return carry

    for yo in range(1, NY):
        first = ((y - yo) % NY) * NZ
        arrive(qo.at[pl.ds(first, NZ)], qoy_r + yo)
    lax.fori_loop(0, NPO, own_pair, 0)
    for c in range(NY):
        obo[c, NZ * NPO * 16:(NZ * NPO + 1) * 16, :] = sto[c].astype(BF16)
    for yo in range(1, NY):
        push(obo.at[(y + yo) % NY], rbo.at[yo - 1], oy_r + yo, ypeer[yo])

    for yo in range(1, NY):
        arrive(frecv.at[yo - 1], fy_r + yo)
    for c in range(2):
        for kind in range(2):
            fsum[c, kind] = fsend[y, c, kind] + frecv[0, c, kind] + frecv[1, c, kind] + frecv[2, c, kind]
    for o in zorder:
        push(fsum.at[((z + o) % NZ) // 4], fz.at[o - 1], fz_r + o, zpeer[o])

    for yo in range(1, NY):
        first = ((y - yo) % NY) * NZ
        arrive(qs.at[pl.ds(first, NZ)], qsy_r + yo)
    lax.fori_loop(0, NPS, taken_pair, 0)
    for c in range(NY):
        obs[c, NZ * NPS * 16:(NZ * NPS + 1) * 16, :] = sts[c].astype(BF16)
    for yo in range(1, NY):
        push(obs.at[(y + yo) % NY], rbs.at[yo - 1], sy_r + yo, ypeer[yo])

    lane16 = lanes((16, HD))

    def merge_y(mine, others, out, pairs):
        at = NZ * pairs * 16
        tiles = [mine[y, at:at + 16, :].astype(F32)]
        tiles += [others[i, at:at + 16, :].astype(F32) for i in range(NY - 1)]
        top, total, factors = merged_stats(tiles, pairs)
        top_high, top_mid = halves(top)
        total_high, total_mid = halves(total)
        phase = lane16 % (4 * pairs)
        stat = jnp.where(
            phase < pairs, top_high,
            jnp.where(
                phase < 2 * pairs, rolled(top_mid, pairs),
                jnp.where(phase < 3 * pairs, rolled(total_high, 2 * pairs), rolled(total_mid, 3 * pairs)),
            ),
        ).astype(BF16)
        for c in range(NZ):
            for p in range(pairs):
                lane = c * 4 * pairs + p
                rows = slice((c * pairs + p) * 16, (c * pairs + p + 1) * 16)
                acc = factors[0][:, lane:lane + 1] * mine[y, rows, :].astype(F32)
                for i in range(NY - 1):
                    acc = acc + factors[i + 1][:, lane:lane + 1] * others[i, rows, :].astype(F32)
                out[c, p * 16:(p + 1) * 16, :] = acc.astype(BF16)
            out[c, pairs * 16:(pairs + 1) * 16, :] = stat

    def merge_z(mine, others, pairs):
        at = pairs * 16
        shift = (128 - z * (4 * pairs)) % 128
        tiles = [mine[z, at:at + 16, :].astype(F32)]
        tiles += [others[i, at:at + 16, :].astype(F32) for i in range(NZ - 1)]
        top, total, factors = merged_stats([pltpu.roll(tile, shift, 1) for tile in tiles], pairs)
        result = []
        for p in range(pairs):
            rows = slice(p * 16, (p + 1) * 16)
            acc = factors[0][:, p:p + 1] * mine[z, rows, :].astype(F32)
            for i in range(NZ - 1):
                acc = acc + factors[i + 1][:, p:p + 1] * others[i, rows, :].astype(F32)
            result.append((acc, top[:, p:p + 1], total[:, p:p + 1]))
        return result

    for yo in range(1, NY):
        arrive(rbo.at[yo - 1], oy_r + yo)
    merge_y(obo, rbo, mbo, NPO)
    for o in zorder:
        push(mbo.at[(z + o) % NZ], zbo.at[o - 1], oz_r + o, zpeer[o])
    for yo in range(1, NY):
        arrive(rbs.at[yo - 1], sy_r + yo)
    merge_y(obs, rbs, mbs, NPS)
    for o in zorder:
        push(mbs.at[(z + o) % NZ], zbs.at[o - 1], sz_r + o, zpeer[o])

    for o in range(1, NZ):
        arrive(fz.at[o - 1], fz_r + o)
    for kind in range(2):
        acc = fsum[z // 4, kind]
        for o in range(1, NZ):
            acc = acc + fz[o - 1, kind]
        fresh[kind] = acc.astype(BF16).astype(F32)

    late = lax.broadcasted_iota(jnp.int32, (8, 1), 0) >= 4

    def finish(r, acc, top, total):
        query = qt[r * 8:(r + 1) * 8]
        tail = [jnp.sum(query * fresh[0, s * 8 + r:s * 8 + r + 1, :], axis=1, keepdims=True) * INV for s in range(2)]
        tail[1] = jnp.where(late, tail[1], MASKED)
        peak = jnp.maximum(top, jnp.maximum(tail[0], tail[1]))
        factor = jnp.exp(top - peak)
        first = jnp.exp(tail[0] - peak)
        second = jnp.where(late, jnp.exp(tail[1] - peak), 0.0)
        total = total * factor + first + second
        acc = acc * factor
        acc = acc + first.astype(BF16).astype(F32) * fresh[1, r:r + 1, :]
        acc = acc + second.astype(BF16).astype(F32) * fresh[1, 8 + r:8 + r + 1, :]
        fin[r * 8:(r + 1) * 8] = acc / total

    for o in range(1, NZ):
        arrive(zbo.at[o - 1], oz_r + o)
    for p, (acc, top, total) in enumerate(merge_z(mbo, zbo, NPO)):
        for i in range(2):
            rows = slice(i * 8, (i + 1) * 8)
            finish(2 * p + i, acc[rows], top[rows], total[rows])

    for o in range(1, NZ):
        arrive(zbs.at[o - 1], sz_r + o)
    lane8 = lanes((8, HD))
    for p, (acc, top, total) in enumerate(merge_z(mbs, zbs, NPS)):
        for i in range(2):
            rows = slice(i * 8, (i + 1) * 8)
            bsend[2 * p + i, 0:8] = acc[rows]
            bsend[2 * p + i, 8:16] = jnp.where(lane8 < 64, top[rows], total[rows])
    for o in range(1, NR):
        push(bsend.at[(me + o) % NR], brecv.at[me], b_r + o, xpeer[o])
    for o in range(1, NR):
        arrive(brecv.at[(me - o) % NR], b_r + o)
    for e in range(STEAL_IN):
        source = plan[me, e, 0]
        tile = brecv[source]
        finish(ROWS + e, tile[0:8], tile[8:16, 0:1], tile[8:16, 64:65])

    for s in range(2):
        for j in range(4):
            out_ref[s, :, j * HD:(j + 1) * HD] = fin[pl.ds(s * 4 + j, ROWS_ALL, stride=8), :].astype(BF16)

    for copy in sends:
        copy.wait_send()


def on_device(kv_pool, page_table, lengths, steal_plan, hidden_rows, kv_weight, queries):
    smem = pl.BlockSpec(memory_space=pltpu.SMEM)
    vmem = pl.BlockSpec(memory_space=pltpu.VMEM)
    hbm = pl.BlockSpec(memory_space=pl.ANY)
    width = 2 * KVH * HD
    tall = lambda n, *lead: pltpu.VMEM((*lead, n, HD), BF16)
    full = lambda n, *lead: pltpu.VMEM((*lead, n, HD), F32)
    out = pl.pallas_call(
        kernel,
        out_shape=jax.ShapeDtypeStruct((2, ROWS_ALL, 512), BF16),
        in_specs=[smem, smem, smem, vmem, vmem, hbm, hbm],
        out_specs=vmem,
        scratch_shapes=[
            pltpu.VMEM((SLOTS, PAGE, width), BF16),
            pltpu.VMEM((SLOTS, PAGE, width), BF16),
            pltpu.VMEM((512, width), BF16),
            full(ROWS_ALL * 8),
            tall(32, NT), tall(64, NT),
            full(8, NR), full(8, NR),
            full(16, NY, 2, 2), full(16, NY - 1, 2, 2), full(16, 2, 2), full(16, NZ - 1, 2), full(16, 2),
            tall((NZ * NPO + 1) * 16, NY), tall((NZ * NPS + 1) * 16, NY),
            tall((NZ * NPO + 1) * 16, NY - 1), tall((NZ * NPS + 1) * 16, NY - 1),
            full(16, NY), full(16, NY),
            tall((NPO + 1) * 16, NZ), tall((NPS + 1) * 16, NZ),
            tall((NPO + 1) * 16, NZ - 1), tall((NPS + 1) * 16, NZ - 1),
            full(16, NR), full(16, NR),
            full(ROWS_ALL * 8),
            pltpu.SemaphoreType.DMA((2,)),
            pltpu.SemaphoreType.DMA((128,)),
            pltpu.SemaphoreType.DMA((96,)),
        ],
        compiler_params=pltpu.CompilerParams(
            collective_id=0, has_side_effects=True, vmem_limit_bytes=48 * 2**20
        ),
    )(page_table[0], lengths, steal_plan, queries[0], hidden_rows[0], kv_pool[0], kv_weight)
    return out[None]


def solution(mesh):
    return jax.shard_map(
        on_device,
        mesh=mesh,
        in_specs=(
            P("replica", "tensor", None, None),
            P("replica", None, "tensor"),
            P(),
            P(),
            P("replica", None, None, "tensor"),
            P("tensor", None),
            P("replica", None, None, "tensor"),
        ),
        out_specs=P("replica", None, None, "tensor"),
        check_vma=False,
    )
```

```python
import functools
import math

import jax
import jax.numpy as jnp
from jax import lax
from jax.experimental import pallas as pl
from jax.experimental.pallas import tpu as pltpu
from jax.sharding import PartitionSpec as P

KVH = 8
HD = 128
PAGE = 32
PPD = 4
STEAL_IN = 3
ROWS = 4
ROWS_ALL = 7
SLOTS = 16
NR = 8
NY = 4
NZ = 8
NT = NY * NZ
MASKED = -1e30
MESH = pl.DeviceIdType.MESH
F32 = jnp.float32
BF16 = jnp.bfloat16
INV = 1.0 / math.sqrt(HD)
NPO = 2
NPS = 4


def lanes(shape):
    return lax.broadcasted_iota(jnp.int32, shape, len(shape) - 1)


def rolled(x, by):
    return pltpu.roll(x, by % 128, 1)


def halves(x):
    high = x.astype(BF16).astype(F32)
    return high, (x - high).astype(BF16).astype(F32)


def merged_stats(tiles, pairs):
    tops, totals = [], []
    for tile in tiles:
        both = tile + rolled(tile, -pairs)
        tops.append(both)
        totals.append(rolled(both, -2 * pairs))
    top = functools.reduce(jnp.maximum, tops)
    factors = [jnp.exp(one - top) for one in tops]
    total = sum(f * l for f, l in zip(factors, totals))
    return top, total, factors


def kernel(
    table_hbm, lengths_hbm, plan_hbm, q_hbm, h_hbm, pool_hbm, w_hbm, out_ref,
    table, lengths, plan, q_ref, h_ref, pool, moved, w, qt, qo, qs, xsend, xrecv, fsend, frecv, fsum, fz, fresh,
    obo, obs, rbo, rbs, sto, sts, mbo, mbs, zbo, zbs, bsend, brecv, fin,
    lsem, ss, rs,
):
    me = lax.axis_index("replica")
    t = lax.axis_index("tensor")
    y, z = t // NZ, t % NZ
    ypeer = [None] + [(me, ((y + o) % NY) * NZ + z) for o in range(1, NY)]
    zpeer = [None] + [(me, y * NZ + (z + o) % NZ) for o in range(1, NZ)]
    xpeer = [None] + [((me + o) % NR, t) for o in range(1, NR)]
    zorder = (1, 7, 2, 6, 3, 5, 4)

    pairs = ((q_hbm, q_ref), (plan_hbm, plan), (h_hbm, h_ref), (w_hbm, w), (pool_hbm, pool), (table_hbm, table), (lengths_hbm, lengths))
    copies = [pltpu.make_async_copy(src, dst, lsem.at[i]) for i, (src, dst) in enumerate(pairs)]
    q_copy, plan_copy, h_copy, w_copy, pool_copy, table_copy, lengths_copy = copies
    for copy in copies:
        copy.start()

    barrier = pltpu.get_barrier_semaphore()
    peers = zpeer[1:] + ypeer[1:] + xpeer[1:]
    for peer in peers:
        pl.semaphore_signal(barrier, inc=1, device_id=peer, device_id_type=MESH)

    q_copy.wait()
    plan_copy.wait()
    for s in range(2):
        for j in range(4):
            qt[pl.ds(s * 4 + j, ROWS_ALL, stride=8), :] = q_ref[:, s, j * HD:(j + 1) * HD].astype(F32)
    qo[t] = qt[0:32].astype(BF16)
    for o in range(1, NR):
        source = (me + o) % NR
        chosen = jnp.zeros((8, HD), F32)
        for e in range(STEAL_IN):
            tile = qt[(ROWS + e) * 8:(ROWS + e + 1) * 8]
            chosen = chosen + jnp.where(plan[e, 0, me] == source, tile, 0.0)
        xsend[o] = chosen
    xrecv[me] = jnp.zeros((8, HD), F32)
    sto[...] = jnp.zeros_like(sto)
    sts[...] = jnp.zeros_like(sts)

    count = [0, 0]
    sends = []

    def fresh_index(kind, n=1):
        first = count[kind]
        count[kind] += n
        return first

    def push(src, dst, recv, peer):
        copy = pltpu.make_async_remote_copy(
            src_ref=src, dst_ref=dst, send_sem=ss.at[fresh_index(0)], recv_sem=rs.at[recv],
            device_id=peer, device_id_type=MESH,
        )
        copy.start()
        sends.append(copy)

    def arrive(dst, recv):
        pltpu.make_async_remote_copy(
            src_ref=dst, dst_ref=dst, send_sem=ss.at[0], recv_sem=rs.at[recv],
            device_id=xpeer[1], device_id_type=MESH,
        ).wait_recv()

    x_r = fresh_index(1, NR)
    qoz_r = fresh_index(1, NZ)
    qoy_r = fresh_index(1, NY)
    qsz_r = fresh_index(1, NZ)
    qsy_r = fresh_index(1, NY)
    fy_r = fresh_index(1, NY)
    fz_r = fresh_index(1, NZ)
    oy_r = fresh_index(1, NY)
    sy_r = fresh_index(1, NY)
    oz_r = fresh_index(1, NZ)
    sz_r = fresh_index(1, NZ)
    b_r = fresh_index(1, NR)

    pl.semaphore_wait(barrier, len(peers))

    for o in range(1, NR):
        push(xsend.at[o], xrecv.at[me], x_r + o, xpeer[o])
    for o in zorder:
        push(qo.at[t], qo.at[t], qoz_r + o, zpeer[o])
    for o in range(1, NY):
        push(qo.at[t], qo.at[t], qoy_r + o, ypeer[o])

    w_copy.wait()
    h_copy.wait()
    hidden = jnp.concatenate(
        [h_ref[:, 0].astype(F32), jnp.zeros((1, 512), F32), h_ref[:, 1].astype(F32), jnp.zeros((1, 512), F32)], axis=0
    ).astype(BF16)
    for kind in range(2):
        for k in range(0, KVH, 2):
            first = (kind * KVH + k) * HD
            part = jnp.dot(hidden, w[:, first:first + 2 * HD], preferred_element_type=F32)
            fsend[k // 2, 0, kind] = part[:, :HD]
            fsend[k // 2, 1, kind] = part[:, HD:]

    def forward(buf, chunk_r, out_r, offsets):
        for o in offsets:
            at = y * NZ + (z - o) % NZ
            arrive(buf.at[at], chunk_r + o)
            for yo in range(1, NY):
                push(buf.at[at], buf.at[at], out_r + yo, ypeer[yo])

    forward(qo, qoz_r, qoy_r, (1, 7))
    for o in range(1, NR):
        arrive(xrecv.at[(me - o) % NR], x_r + o)
    qs[t] = xrecv[...].reshape(NR * 8, HD).astype(BF16)
    for o in zorder:
        push(qs.at[t], qs.at[t], qsz_r + o, zpeer[o])
    forward(qo, qoz_r, qoy_r, (2, 6, 3, 5, 4))
    for yo in range(1, NY):
        push(qs.at[t], qs.at[t], qsy_r + yo, ypeer[yo])

    row_id = lax.broadcasted_iota(jnp.int32, (HD, HD), 0)
    both = jnp.bitwise_and(row_id, lanes((HD, HD)))
    parity = jnp.zeros((HD, HD), jnp.int32)
    for bit in range(7):
        parity = parity + jnp.bitwise_and(jnp.right_shift(both, bit), 1)
    signs = (1.0 - 2.0 * jnp.bitwise_and(parity, 1).astype(F32)).astype(BF16)

    pool_copy.wait()
    table_copy.wait()
    lengths_copy.wait()

    def round_trip(slot, carry):
        page = pool[slot]
        rows = jnp.concatenate([page[:, i * HD:(i + 1) * HD] for i in range(2 * KVH)], axis=0)
        turned = jnp.dot(rows, signs, preferred_element_type=F32) * INV
        scales = (jnp.max(jnp.abs(turned), axis=1, keepdims=True) + 1e-06).astype(BF16).astype(F32)
        packed = (turned * (1.0 / scales)).astype(BF16)
        back = (jnp.dot(packed, signs, preferred_element_type=F32) * (scales * INV)).astype(BF16)
        for i in range(2 * KVH):
            moved[slot, :, i * HD:(i + 1) * HD] = back[i * PAGE:(i + 1) * PAGE]
        return carry

    lax.fori_loop(0, SLOTS // 2, round_trip, 0, unroll=4)
    forward(qs, qsz_r, qsy_r, (1, 7, 2, 6, 3, 5, 4))
    for yo in range(1, NY):
        push(fsend.at[(y + yo) % NY], frecv.at[yo - 1], fy_r + yo, ypeer[yo])
    lax.fori_loop(SLOTS // 2, SLOTS, round_trip, 0, unroll=4)

    row16 = lax.broadcasted_iota(jnp.int32, (64, HD), 0) % 16
    lane64 = lanes((64, HD))
    first_half = row16 < 8
    mask_a = jnp.where(first_half, 1.0, 0.0).astype(BF16)
    mask_b = jnp.where(first_half, 0.0, 1.0).astype(BF16)
    place = ((lane64 // PAGE) * NT + t) * PAGE + lane64 % PAGE
    dest = lax.broadcasted_iota(jnp.int32, (64, HD), 0) // 16

    def attend(pages, queries, results, stats, pairs, describe, p):
        (slots_a, span_a), (slots_b, span_b) = describe(2 * p), describe(2 * p + 1)
        valid = place < jnp.where(first_half, span_a, span_b)
        at = pl.multiple_of(p * 16, 16)

        def tokens(slots, first):
            return jnp.concatenate([pages[slot, :, first:first + HD] for slot in slots], axis=0)

        scores, tops, lights, totals, mixed = [], [], [], [], []
        for k in range(KVH):
            query = queries[4 * k:4 * k + 4, pl.ds(at, 16), :].reshape(64, HD)
            wide = jnp.concatenate([query * mask_a, query * mask_b], axis=1)
            keys = jnp.concatenate([tokens(slots_a, k * HD), tokens(slots_b, k * HD)], axis=1)
            scores.append(lax.dot_general(wide, keys, (((1,), (1,)), ((), ())), preferred_element_type=F32))
        for k in range(KVH):
            scores[k] = jnp.where(valid, scores[k] * INV, MASKED)
            tops.append(halves(jnp.max(scores[k], axis=1, keepdims=True)))
        for k in range(KVH):
            weights = jnp.where(valid, jnp.exp(scores[k] - (tops[k][0] + tops[k][1])), 0.0)
            totals.append(halves(jnp.sum(weights, axis=1, keepdims=True)))
            lights.append(weights.astype(BF16))
        for k in range(KVH):
            wide = jnp.concatenate([lights[k] * mask_a, lights[k] * mask_b], axis=1)
            values = jnp.concatenate(
                [tokens(slots_a, (KVH + k) * HD), tokens(slots_b, (KVH + k) * HD)], axis=0
            )
            mixed.append(jnp.dot(wide, values, preferred_element_type=F32).astype(BF16))
        for k in range(KVH):
            for j in range(4):
                where = pl.multiple_of(((4 * (k % 2) + j) * pairs + p) * 16, 16)
                results[k // 2, pl.ds(where, 16), :] = mixed[k][j * 16:(j + 1) * 16]
        for c in range(KVH // 2):
            sums = stats[c]
            for k in (2 * c, 2 * c + 1):
                lane = lane64 - (4 * (k % 2) + dest) * (4 * pairs) - p
                tile = jnp.where(lane == 0, tops[k][0], 0.0)
                tile = jnp.where(lane == pairs, tops[k][1], tile)
                tile = jnp.where(lane == 2 * pairs, totals[k][0], tile)
                tile = jnp.where(lane == 3 * pairs, totals[k][1], tile)
                sums = sums + jnp.sum(tile.reshape(4, 16, HD), axis=0)
            stats[c] = sums

    def own(r):
        return [table[r, j] for j in range(PPD)], lengths[r, me]

    def taken(d):
        request = jnp.int32(0)
        for e in range(STEAL_IN):
            request = request + jnp.where(plan[e, 0, d] == me, plan[e, 1, d], 0)
        return [table[request, j] for j in range(PPD)], lengths[request, me]

    def own_pair(p, carry):
        attend(pool, qo, obo, sto, NPO, own, p)
        return carry

    def taken_pair(p, carry):
        attend(moved, qs, obs, sts, NPS, taken, p)
        return carry

    for yo in range(1, NY):
        first = ((y - yo) % NY) * NZ
        arrive(qo.at[pl.ds(first, NZ)], qoy_r + yo)
    lax.fori_loop(0, NPO, own_pair, 0)
    for c in range(NY):
        obo[c, NZ * NPO * 16:(NZ * NPO + 1) * 16, :] = sto[c].astype(BF16)
    for yo in range(1, NY):
        push(obo.at[(y + yo) % NY], rbo.at[yo - 1], oy_r + yo, ypeer[yo])

    for yo in range(1, NY):
        arrive(frecv.at[yo - 1], fy_r + yo)
    for c in range(2):
        for kind in range(2):
            fsum[c, kind] = fsend[y, c, kind] + frecv[0, c, kind] + frecv[1, c, kind] + frecv[2, c, kind]
    for o in zorder:
        push(fsum.at[((z + o) % NZ) // 4], fz.at[o - 1], fz_r + o, zpeer[o])

    for yo in range(1, NY):
        first = ((y - yo) % NY) * NZ
        arrive(qs.at[pl.ds(first, NZ)], qsy_r + yo)
    lax.fori_loop(0, NPS, taken_pair, 0)
    for c in range(NY):
        obs[c, NZ * NPS * 16:(NZ * NPS + 1) * 16, :] = sts[c].astype(BF16)
    for yo in range(1, NY):
        push(obs.at[(y + yo) % NY], rbs.at[yo - 1], sy_r + yo, ypeer[yo])

    lane16 = lanes((16, HD))

    def merge_y(mine, others, out, pairs):
        at = NZ * pairs * 16
        tiles = [mine[y, at:at + 16, :].astype(F32)]
        tiles += [others[i, at:at + 16, :].astype(F32) for i in range(NY - 1)]
        top, total, factors = merged_stats(tiles, pairs)
        top_high, top_mid = halves(top)
        total_high, total_mid = halves(total)
        phase = lane16 % (4 * pairs)
        stat = jnp.where(
            phase < pairs, top_high,
            jnp.where(
                phase < 2 * pairs, rolled(top_mid, pairs),
                jnp.where(phase < 3 * pairs, rolled(total_high, 2 * pairs), rolled(total_mid, 3 * pairs)),
            ),
        ).astype(BF16)
        for c in range(NZ):
            for p in range(pairs):
                lane = c * 4 * pairs + p
                rows = slice((c * pairs + p) * 16, (c * pairs + p + 1) * 16)
                acc = factors[0][:, lane:lane + 1] * mine[y, rows, :].astype(F32)
                for i in range(NY - 1):
                    acc = acc + factors[i + 1][:, lane:lane + 1] * others[i, rows, :].astype(F32)
                out[c, p * 16:(p + 1) * 16, :] = acc.astype(BF16)
            out[c, pairs * 16:(pairs + 1) * 16, :] = stat

    def merge_z(mine, others, pairs):
        at = pairs * 16
        shift = (128 - z * (4 * pairs)) % 128
        tiles = [mine[z, at:at + 16, :].astype(F32)]
        tiles += [others[i, at:at + 16, :].astype(F32) for i in range(NZ - 1)]
        top, total, factors = merged_stats([pltpu.roll(tile, shift, 1) for tile in tiles], pairs)
        result = []
        for p in range(pairs):
            rows = slice(p * 16, (p + 1) * 16)
            acc = factors[0][:, p:p + 1] * mine[z, rows, :].astype(F32)
            for i in range(NZ - 1):
                acc = acc + factors[i + 1][:, p:p + 1] * others[i, rows, :].astype(F32)
            result.append((acc, top[:, p:p + 1], total[:, p:p + 1]))
        return result

    for yo in range(1, NY):
        arrive(rbo.at[yo - 1], oy_r + yo)
    merge_y(obo, rbo, mbo, NPO)
    for o in zorder:
        push(mbo.at[(z + o) % NZ], zbo.at[o - 1], oz_r + o, zpeer[o])
    for yo in range(1, NY):
        arrive(rbs.at[yo - 1], sy_r + yo)
    merge_y(obs, rbs, mbs, NPS)
    for o in zorder:
        push(mbs.at[(z + o) % NZ], zbs.at[o - 1], sz_r + o, zpeer[o])

    for o in range(1, NZ):
        arrive(fz.at[o - 1], fz_r + o)
    for kind in range(2):
        acc = fsum[z // 4, kind]
        for o in range(1, NZ):
            acc = acc + fz[o - 1, kind]
        fresh[kind] = acc.astype(BF16).astype(F32)

    late = lax.broadcasted_iota(jnp.int32, (8, 1), 0) >= 4

    def finish(r, acc, top, total):
        query = qt[r * 8:(r + 1) * 8]
        tail = [jnp.sum(query * fresh[0, s * 8 + r:s * 8 + r + 1, :], axis=1, keepdims=True) * INV for s in range(2)]
        tail[1] = jnp.where(late, tail[1], MASKED)
        peak = jnp.maximum(top, jnp.maximum(tail[0], tail[1]))
        factor = jnp.exp(top - peak)
        first = jnp.exp(tail[0] - peak)
        second = jnp.where(late, jnp.exp(tail[1] - peak), 0.0)
        total = total * factor + first + second
        acc = acc * factor
        acc = acc + first.astype(BF16).astype(F32) * fresh[1, r:r + 1, :]
        acc = acc + second.astype(BF16).astype(F32) * fresh[1, 8 + r:8 + r + 1, :]
        fin[r * 8:(r + 1) * 8] = acc / total

    for o in range(1, NZ):
        arrive(zbo.at[o - 1], oz_r + o)
    for p, (acc, top, total) in enumerate(merge_z(mbo, zbo, NPO)):
        for i in range(2):
            rows = slice(i * 8, (i + 1) * 8)
            finish(2 * p + i, acc[rows], top[rows], total[rows])

    for o in range(1, NZ):
        arrive(zbs.at[o - 1], sz_r + o)
    lane8 = lanes((8, HD))
    for p, (acc, top, total) in enumerate(merge_z(mbs, zbs, NPS)):
        for i in range(2):
            rows = slice(i * 8, (i + 1) * 8)
            bsend[2 * p + i, 0:8] = acc[rows]
            bsend[2 * p + i, 8:16] = jnp.where(lane8 < 64, top[rows], total[rows])
    for o in range(1, NR):
        push(bsend.at[(me + o) % NR], brecv.at[me], b_r + o, xpeer[o])
    for o in range(1, NR):
        arrive(brecv.at[(me - o) % NR], b_r + o)
    for e in range(STEAL_IN):
        source = plan[e, 0, me]
        tile = brecv[source]
        finish(ROWS + e, tile[0:8], tile[8:16, 0:1], tile[8:16, 64:65])

    for s in range(2):
        for j in range(4):
            out_ref[:, s, j * HD:(j + 1) * HD] = fin[pl.ds(s * 4 + j, ROWS_ALL, stride=8), :].astype(BF16)

    for copy in sends:
        copy.wait_send()


def on_device(kv_pool, page_table, lengths, steal_plan, hidden_rows, kv_weight, queries):
    vmem = pl.BlockSpec(memory_space=pltpu.VMEM)
    hbm = pl.BlockSpec(memory_space=pltpu.HBM)
    width = 2 * KVH * HD
    tall = lambda n, *lead: pltpu.VMEM((*lead, n, HD), BF16)
    full = lambda n, *lead: pltpu.VMEM((*lead, n, HD), F32)
    out = pl.pallas_call(
        kernel,
        out_shape=jax.ShapeDtypeStruct((ROWS_ALL, 2, 512), BF16),
        in_specs=[hbm] * 7,
        out_specs=vmem,
        scratch_shapes=[
            pltpu.SMEM((ROWS, PPD), jnp.int32),
            pltpu.SMEM((ROWS, NR), jnp.int32),
            pltpu.SMEM((STEAL_IN, 2, NR), jnp.int32),
            pltpu.VMEM((ROWS_ALL, 2, 512), BF16),
            pltpu.VMEM((ROWS_ALL, 2, 512), BF16),
            pltpu.VMEM((SLOTS, PAGE, width), BF16),
            pltpu.VMEM((SLOTS, PAGE, width), BF16),
            pltpu.VMEM((512, width), BF16),
            full(ROWS_ALL * 8),
            tall(32, NT), tall(64, NT),
            full(8, NR), full(8, NR),
            full(16, NY, 2, 2), full(16, NY - 1, 2, 2), full(16, 2, 2), full(16, NZ - 1, 2), full(16, 2),
            tall((NZ * NPO + 1) * 16, NY), tall((NZ * NPS + 1) * 16, NY),
            tall((NZ * NPO + 1) * 16, NY - 1), tall((NZ * NPS + 1) * 16, NY - 1),
            full(16, NY), full(16, NY),
            tall((NPO + 1) * 16, NZ), tall((NPS + 1) * 16, NZ),
            tall((NPO + 1) * 16, NZ - 1), tall((NPS + 1) * 16, NZ - 1),
            full(16, NR), full(16, NR),
            full(ROWS_ALL * 8),
            pltpu.SemaphoreType.DMA((7,)),
            pltpu.SemaphoreType.DMA((128,)),
            pltpu.SemaphoreType.DMA((96,)),
        ],
        compiler_params=pltpu.CompilerParams(
            collective_id=0, has_side_effects=True, vmem_limit_bytes=63 * 2**20
        ),
    )(
        page_table[0], lengths.T, steal_plan.transpose(1, 2, 0), queries[0].transpose(1, 0, 2),
        hidden_rows[0].transpose(1, 0, 2), kv_pool[0], kv_weight,
    )
    return out.transpose(1, 0, 2)[None]


def solution(mesh):
    return jax.shard_map(
        on_device,
        mesh=mesh,
        in_specs=(
            P("replica", "tensor", None, None),
            P("replica", None, "tensor"),
            P(),
            P(),
            P("replica", None, None, "tensor"),
            P("tensor", None),
            P("replica", None, None, "tensor"),
        ),
        out_specs=P("replica", None, None, "tensor"),
        check_vma=False,
    )
```

```python
import functools
import math

import jax
import jax.numpy as jnp
from jax import lax
from jax.experimental import pallas as pl
from jax.experimental.pallas import tpu as pltpu
from jax.sharding import PartitionSpec as P

KVH = 8
HD = 128
PAGE = 32
PPD = 4
STEAL_IN = 3
ROWS = 4
ROWS_ALL = 7
SLOTS = 16
NR = 8
NY = 4
NZ = 8
NT = NY * NZ
MASKED = -1e30
MESH = pl.DeviceIdType.MESH
F32 = jnp.float32
BF16 = jnp.bfloat16
INV = 1.0 / math.sqrt(HD)
OWN = ROWS * 64 + 16
ONE = 64 + 16


def lanes(shape):
    return lax.broadcasted_iota(jnp.int32, shape, len(shape) - 1)


def halves(x):
    high = x.astype(BF16).astype(F32)
    return high, (x - high).astype(BF16).astype(F32)


def stat_factors(tiles):
    tops = [tile + pltpu.roll(tile, 127, 1) for tile in tiles]
    totals = [pltpu.roll(one, 126, 1) for one in tops]
    top = functools.reduce(jnp.maximum, tops)
    factors = [jnp.exp(one - top) for one in tops]
    total = sum(f * l for f, l in zip(factors, totals))
    return top, total, factors


def column(x, first):
    return jnp.concatenate([x[:, first + 4 * g:first + 4 * g + 1] for g in range(4)], axis=0)


def merged(stat, first, parts):
    top, total, factors = stat
    acc = sum(column(f, first) * part.astype(F32) for f, part in zip(factors, parts))
    return acc, column(top, first), column(total, first)


def kernel(
    table_hbm, lengths_hbm, plan_hbm, q_hbm, h_hbm, pool_hbm, w_hbm, out_ref,
    table, lengths, plan, q_ref, h_ref, pool, moved, w, qt, qz, qown, qsend, qslot,
    fsend, frecv, fsum, fz, fresh, obo, rbo, obs, rbs, sto, macc, mst, mb, zb, fin,
    lsem, ss, rs, slot_rs,
):
    me = lax.axis_index("replica")
    t = lax.axis_index("tensor")
    y, z = t // NZ, t % NZ

    def near(o=0, yo=0, zo=0):
        return ((me + o) % NR, ((y + yo) % NY) * NZ + (z + zo) % NZ)

    zorder = (4, 3, 5, 2, 6, 1, 7)

    pairs = (
        (q_hbm, q_ref), (plan_hbm, plan), (h_hbm, h_ref), (w_hbm, w),
        (pool_hbm, pool), (table_hbm, table), (lengths_hbm, lengths),
    )
    copies = [pltpu.make_async_copy(src, dst, lsem.at[i]) for i, (src, dst) in enumerate(pairs)]
    q_copy, plan_copy, h_copy, w_copy, pool_copy, table_copy, lengths_copy = copies
    for copy in copies:
        copy.start()

    barrier = pltpu.get_barrier_semaphore()
    peers = [near(zo=o) for o in zorder] + [near(yo=o) for o in range(1, NY)]
    peers += [near(o, yo) for o in range(1, NR) for yo in range(NY)]
    for peer in peers:
        pl.semaphore_signal(barrier, inc=1, device_id=peer, device_id_type=MESH)

    q_copy.wait()
    for s in range(2):
        for j in range(4):
            qt[pl.ds(s * 4 + j, ROWS_ALL, stride=8), :] = q_ref[:, s, j * HD:(j + 1) * HD].astype(F32)
    qt[56:64] = jnp.zeros((8, HD), F32)
    qz[0] = qt[...].astype(BF16)
    qslot[NR - 1] = jnp.zeros((NY, 64, HD), BF16)
    sto[...] = jnp.zeros_like(sto)
    mst[...] = jnp.zeros_like(mst)

    def push(src, dst, stage, peer, recv=None):
        pltpu.make_async_remote_copy(
            src_ref=src, dst_ref=dst, send_sem=ss.at[stage], recv_sem=rs.at[stage] if recv is None else recv,
            device_id=peer, device_id_type=MESH,
        ).start()

    def whole(ref, stage, recv=None):
        return pltpu.make_async_remote_copy(
            src_ref=ref, dst_ref=ref, send_sem=ss.at[stage], recv_sem=rs.at[stage] if recv is None else recv,
            device_id=near(1), device_id_type=MESH,
        )

    QZ, QY, QX, FY, FZ, OY, OX, OZ = range(8)

    pl.semaphore_wait(barrier, len(peers))

    for o in zorder:
        push(qz.at[0], qz.at[o], QZ, near(zo=o))

    w_copy.wait()
    h_copy.wait()
    gap = jnp.zeros((1, 512), F32)
    hidden = jnp.concatenate([h_ref[:, 0].astype(F32), gap, h_ref[:, 1].astype(F32), gap], axis=0).astype(BF16)
    for kind in range(2):
        for k in range(0, KVH, 2):
            first = (kind * KVH + k) * HD
            part = jnp.dot(hidden, w[:, first:first + 2 * HD], preferred_element_type=F32)
            fsend[k // 2, 0, kind] = part[:, :HD]
            fsend[k // 2, 1, kind] = part[:, HD:]
    for yo in range(1, NY):
        push(fsend.at[(y + yo) % NY], frecv.at[yo - 1], FY, near(yo=yo))

    plan_copy.wait()
    whole(qz.at[1:NZ], QZ).wait_recv()
    chunks = [qz[(z - c + NZ) % NZ].astype(F32) for c in range(NZ)]

    def by_row(r):
        return jnp.concatenate([chunk[r * 8:(r + 1) * 8] for chunk in chunks], axis=0)

    for r in range(ROWS):
        qown[0, r] = by_row(r).astype(BF16)
    for yo in range(1, NY):
        push(qown.at[0], qown.at[yo], QY, near(yo=yo))
    leaving = [by_row(ROWS + e) for e in range(STEAL_IN)]
    for o in range(1, NR):
        source = (me - o + NR) % NR
        chosen = jnp.zeros((64, HD), F32)
        for e in range(STEAL_IN):
            chosen = chosen + jnp.where(plan[e, 0, me] == source, leaving[e], 0.0)
        qsend[o - 1] = chosen.astype(BF16)
        for yo in range(NY):
            push(qsend.at[o - 1], qslot.at[o - 1, yo], QX, near(-o + NR, yo), slot_rs.at[(o - 1) // 2])

    row_id = lax.broadcasted_iota(jnp.int32, (HD, HD), 0)
    both = jnp.bitwise_and(row_id, lanes((HD, HD)))
    parity = jnp.zeros((HD, HD), jnp.int32)
    for bit in range(7):
        parity = parity + jnp.bitwise_and(jnp.right_shift(both, bit), 1)
    signs = (1.0 - 2.0 * jnp.bitwise_and(parity, 1).astype(F32)).astype(BF16)

    pool_copy.wait()
    table_copy.wait()
    lengths_copy.wait()

    def round_trip(slot, carry):
        page = pool[slot]
        rows = jnp.concatenate([page[:, i * HD:(i + 1) * HD] for i in range(2 * KVH)], axis=0)
        turned = jnp.dot(rows, signs, preferred_element_type=F32) * INV
        scales = (jnp.max(jnp.abs(turned), axis=1, keepdims=True) + 1e-06).astype(BF16).astype(F32)
        packed = (turned * (1.0 / scales)).astype(BF16)
        back = (jnp.dot(packed, signs, preferred_element_type=F32) * (scales * INV)).astype(BF16)
        for i in range(2 * KVH):
            moved[slot, :, i * HD:(i + 1) * HD] = back[i * PAGE:(i + 1) * PAGE]
        return carry

    lax.fori_loop(0, SLOTS, round_trip, 0, unroll=4)

    lane64 = lanes((64, HD))
    row64 = lax.broadcasted_iota(jnp.int32, (64, HD), 0)
    upper = row64 < 32
    place = ((lane64 // PAGE) * NT + t) * PAGE + lane64 % PAGE
    blank = jnp.zeros((32, HD), BF16)

    def attend(pages, a, b, query, put, put_stats, lane_a, lane_b):
        (slots_a, span_a), (slots_b, span_b) = a, b
        valid = place < jnp.where(upper, span_a, span_b)

        def tokens(slots, first):
            return jnp.concatenate([pages[slot, :, first:first + HD] for slot in slots], axis=0)

        def spread(first, second):
            return jnp.concatenate(
                [jnp.concatenate([first, blank], axis=1), jnp.concatenate([blank, second], axis=1)], axis=0
            )

        scores, tops, lights, totals, mixed = [], [], [], [], []
        for k in range(KVH):
            wide = spread(query(0, k), query(1, k))
            keys = jnp.concatenate([tokens(slots_a, k * HD), tokens(slots_b, k * HD)], axis=1)
            scores.append(lax.dot_general(wide, keys, (((1,), (1,)), ((), ())), preferred_element_type=F32))
        for k in range(KVH):
            scores[k] = jnp.where(valid, scores[k] * INV, MASKED)
            tops.append(halves(jnp.max(scores[k], axis=1, keepdims=True)))
        for k in range(KVH):
            weights = jnp.where(valid, jnp.exp(scores[k] - (tops[k][0] + tops[k][1])), 0.0)
            totals.append(halves(jnp.sum(weights, axis=1, keepdims=True)))
            lights.append(weights.astype(BF16))
        for k in range(KVH):
            wide = spread(lights[k][:32], lights[k][32:])
            values = jnp.concatenate(
                [tokens(slots_a, (KVH + k) * HD), tokens(slots_b, (KVH + k) * HD)], axis=0
            )
            mixed.append(jnp.dot(wide, values, preferred_element_type=F32).astype(BF16))
        for k in range(KVH):
            put(0, k, mixed[k][:32])
            put(1, k, mixed[k][32:])
        shift = (row64 % 32) // 16 * 4 + jnp.where(upper, lane_a, lane_b)
        for c in range(KVH // 2):
            tile = jnp.zeros((64, HD), F32)
            for k in (2 * c, 2 * c + 1):
                lane = lane64 - shift - 8 * (k % 2)
                for i, piece in enumerate(tops[k] + totals[k]):
                    tile = jnp.where(lane == i, piece, tile)
            put_stats(0, c, tile[:16] + tile[16:32])
            put_stats(1, c, tile[32:48] + tile[48:])

    def pages_of(request):
        return [table[request, j] for j in range(PPD)], lengths[request, me]

    def own_pair(p, carry):
        def put(i, k, value):
            at = pl.multiple_of((2 * p + i) * 64 + (k % 2) * 32, 32)
            obo[k // 2, pl.ds(at, 32), :] = value

        def put_stats(i, c, tile):
            sto[c] = sto[c] + tile

        def query(i, k):
            return qown[(y - k // 2 + NY) % NY, 2 * p + i, (k % 2) * 32:(k % 2 + 1) * 32, :]

        attend(pool, pages_of(2 * p), pages_of(2 * p + 1), query, put, put_stats, 32 * p, 32 * p + 16)
        return carry

    def taken(o):
        taker = (me + o + 1) % NR
        request = jnp.int32(0)
        for e in range(STEAL_IN):
            request = request + jnp.where(plan[e, 0, taker] == me, plan[e, 1, taker], 0)
        return pages_of(request)

    def taken_pair(p, carry):
        def put(i, k, value):
            obs[2 * p + i, k // 2, (k % 2) * 32:(k % 2 + 1) * 32, :] = value

        def put_stats(i, c, tile):
            obs[2 * p + i, c, 64:80, :] = tile.astype(BF16)

        def query(i, k):
            return qslot[2 * p + i, (y - k // 2 + NY) % NY, (k % 2) * 32:(k % 2 + 1) * 32, :]

        attend(moved, taken(2 * p), taken(2 * p + 1), query, put, put_stats, 0, 0)
        return carry

    whole(qown.at[1:NY], QY).wait_recv()
    lax.fori_loop(0, ROWS // 2, own_pair, 0)
    for c in range(NY):
        obo[c, ROWS * 64:OWN, :] = sto[c].astype(BF16)
    for yo in range(1, NY):
        push(obo.at[(y + yo) % NY], rbo.at[yo - 1], OY, near(yo=yo))

    whole(frecv, FY).wait_recv()
    for c in range(2):
        for kind in range(2):
            fsum[c, kind] = fsend[y, c, kind] + frecv[0, c, kind] + frecv[1, c, kind] + frecv[2, c, kind]
    for o in zorder:
        push(fsum.at[((z + o) % NZ) // 4], fz.at[o - 1], FZ, near(zo=o))

    for p in range(NR // 2):
        whole(qslot.at[2 * p:min(2 * p + 2, NR - 1)], QX, slot_rs.at[p]).wait_recv()
        taken_pair(p, 0)
        for o in range(2 * p + 1, min(2 * p + 3, NR)):
            for yo in range(NY):
                push(obs.at[o - 1, (y + yo) % NY], rbs.at[o - 1, yo], OX, near(o, yo))

    def keep(r, acc, top, total):
        macc[r] = acc
        tile = jnp.zeros((64, HD), F32)
        for i, piece in enumerate(halves(top) + halves(total)):
            tile = jnp.where(lane64 == r // 2 * 4 + i, piece, tile)
        mst[r % 2] = mst[r % 2] + tile

    whole(rbo, OY).wait_recv()
    held = [obo.at[y]] + [rbo.at[i] for i in range(NY - 1)]
    stat = stat_factors([ref[ROWS * 64:OWN, :].astype(F32) for ref in held])
    for r in range(ROWS):
        keep(r, *merged(stat, 16 * r, [ref[r * 64:(r + 1) * 64, :] for ref in held]))

    whole(rbs, OX).wait_recv()
    for e in range(STEAL_IN):
        o = jnp.minimum((me - plan[e, 0, me] + 2 * NR - 1) % NR, NR - 2)
        parts = [rbs[o, i] for i in range(NY)]
        stat = stat_factors([part[64:].astype(F32) for part in parts])
        keep(ROWS + e, *merged(stat, 0, [part[:64] for part in parts]))

    for c in range(NZ):
        rows = slice(c * 8, (c + 1) * 8)
        mb[c, 0:64, :] = jnp.concatenate(
            [macc[r, rows, :] for r in range(ROWS_ALL)] + [jnp.zeros((8, HD), F32)], axis=0
        ).astype(BF16)
        mb[c, 64:80, :] = jnp.concatenate([mst[0, rows, :], mst[1, rows, :]], axis=0).astype(BF16)
    for o in zorder:
        push(mb.at[(z + o) % NZ], zb.at[o - 1], OZ, near(zo=o))

    whole(fz, FZ).wait_recv()
    for kind in range(2):
        acc = fsum[z // 4, kind]
        for o in range(1, NZ):
            acc = acc + fz[o - 1, kind]
        fresh[kind] = acc.astype(BF16).astype(F32)

    def new_rows(kind, s):
        return jnp.concatenate(
            [jnp.broadcast_to(fresh[kind, s * 8 + r:s * 8 + r + 1, :], (8, HD)) for r in range(8)], axis=0
        )

    late = lax.broadcasted_iota(jnp.int32, (64, 1), 0) % 8 >= 4
    query = qt[...]
    tail = [jnp.sum(query * new_rows(0, s), axis=1, keepdims=True) * INV for s in range(2)]
    tail[1] = jnp.where(late, tail[1], MASKED)
    tail_top = jnp.maximum(tail[0], tail[1])

    whole(zb, OZ).wait_recv()
    held = [mb.at[z]] + [zb.at[i] for i in range(NZ - 1)]
    stat = stat_factors([ref[64:ONE, :].astype(F32) for ref in held])
    acc, top, total = merged(stat, 0, [ref[0:64, :] for ref in held])
    peak = jnp.maximum(top, tail_top)
    factor = jnp.exp(top - peak)
    first = jnp.exp(tail[0] - peak)
    second = jnp.where(late, jnp.exp(tail[1] - peak), 0.0)
    total = total * factor + first + second
    acc = acc * factor
    acc = acc + first.astype(BF16).astype(F32) * new_rows(1, 0)
    acc = acc + second.astype(BF16).astype(F32) * new_rows(1, 1)
    fin[...] = acc / total
    for s in range(2):
        for j in range(4):
            out_ref[:, s, j * HD:(j + 1) * HD] = fin[pl.ds(s * 4 + j, ROWS_ALL, stride=8), :].astype(BF16)

    whole(qz.at[1:NZ], QZ).wait_send()
    whole(frecv, FY).wait_send()
    whole(qown.at[1:NY], QY).wait_send()
    whole(qslot.at[0:NR - 1], QX).wait_send()
    whole(rbo, OY).wait_send()
    whole(fz, FZ).wait_send()
    whole(rbs, OX).wait_send()
    whole(zb, OZ).wait_send()


def on_device(kv_pool, page_table, lengths, steal_plan, hidden_rows, kv_weight, queries):
    hbm = pl.BlockSpec(memory_space=pltpu.HBM)
    width = 2 * KVH * HD

    def half(*shape):
        return pltpu.VMEM((*shape, HD), BF16)

    def full(*shape):
        return pltpu.VMEM((*shape, HD), F32)

    out = pl.pallas_call(
        kernel,
        out_shape=jax.ShapeDtypeStruct((ROWS_ALL, 2, 512), BF16),
        in_specs=[hbm] * 7,
        out_specs=pl.BlockSpec(memory_space=pltpu.VMEM),
        scratch_shapes=[
            pltpu.SMEM((ROWS, PPD), jnp.int32),
            pltpu.SMEM((ROWS, NR), jnp.int32),
            pltpu.SMEM((STEAL_IN, 2, NR), jnp.int32),
            pltpu.VMEM((ROWS_ALL, 2, 512), BF16),
            pltpu.VMEM((ROWS_ALL, 2, 512), BF16),
            pltpu.VMEM((SLOTS, PAGE, width), BF16),
            pltpu.VMEM((SLOTS, PAGE, width), BF16),
            pltpu.VMEM((512, width), BF16),
            full(64), half(NZ, 64), half(NY, ROWS, 64), half(NR - 1, 64), half(NR, NY, 64),
            full(NY, 2, 2, 16), full(NY - 1, 2, 2, 16), full(2, 2, 16), full(NZ - 1, 2, 16), full(2, 16),
            half(NY, OWN), half(NY - 1, OWN), half(NR, NY, ONE), half(NR - 1, NY, ONE),
            full(NY, 16), full(ROWS_ALL, 64), full(2, 64), half(NZ, ONE), half(NZ - 1, ONE), full(64),
            pltpu.SemaphoreType.DMA((7,)),
            pltpu.SemaphoreType.DMA((8,)),
            pltpu.SemaphoreType.DMA((8,)),
            pltpu.SemaphoreType.DMA((NR // 2,)),
        ],
        compiler_params=pltpu.CompilerParams(
            collective_id=0, has_side_effects=True, vmem_limit_bytes=63 * 2**20
        ),
    )(
        page_table[0], lengths.T, steal_plan.transpose(1, 2, 0), queries[0].transpose(1, 0, 2),
        hidden_rows[0].transpose(1, 0, 2), kv_pool[0], kv_weight,
    )
    return out.transpose(1, 0, 2)[None]


def solution(mesh):
    return jax.shard_map(
        on_device,
        mesh=mesh,
        in_specs=(
            P("replica", "tensor", None, None),
            P("replica", None, "tensor"),
            P(),
            P(),
            P("replica", None, None, "tensor"),
            P("tensor", None),
            P("replica", None, None, "tensor"),
        ),
        out_specs=P("replica", None, None, "tensor"),
        check_vma=False,
    )
```

```python
import functools
import math

import jax
import jax.numpy as jnp
from jax import lax
from jax.experimental import pallas as pl
from jax.experimental.pallas import tpu as pltpu
from jax.sharding import PartitionSpec as P

KVH = 8
HD = 128
PAGE = 32
PPD = 4
STEAL_IN = 3
ROWS = 4
ROWS_ALL = 7
SLOTS = 16
NR = 8
NY = 4
NZ = 8
NT = NY * NZ
MASKED = -1e30
MESH = pl.DeviceIdType.MESH
F32 = jnp.float32
BF16 = jnp.bfloat16
INV = 1.0 / math.sqrt(HD)
OWN = NY * ROWS * 8 + 16
ONE = 64 + 16
LAST = 32 + 16


def lanes(shape):
    return lax.broadcasted_iota(jnp.int32, shape, len(shape) - 1)


def halves(x):
    high = x.astype(BF16).astype(F32)
    return high, (x - high).astype(BF16).astype(F32)


def stat_factors(tiles):
    tops = [tile + pltpu.roll(tile, 127, 1) for tile in tiles]
    totals = [pltpu.roll(one, 126, 1) for one in tops]
    top = functools.reduce(jnp.maximum, tops)
    factors = [jnp.exp(one - top) for one in tops]
    total = sum(f * l for f, l in zip(factors, totals))
    return top, total, factors


def column(x, groups):
    return jnp.concatenate([x[:, 4 * g:4 * g + 1] for g in range(groups)], axis=0)


def merged(held, rows):
    groups = rows // 16
    top, total, factors = stat_factors([part[rows:rows + 16].astype(F32) for part in held])
    acc = sum(column(f, groups) * part[:rows].astype(F32) for f, part in zip(factors, held))
    return acc, column(top, groups), column(total, groups)


def kernel(
    table_hbm, lengths_hbm, plan_hbm, q_hbm, h_hbm, pool_hbm, w_hbm, out_ref,
    table, lengths, plan, q_ref, h_ref, pool, moved, w, qt, qz, qyz, qown, qsend, qslot,
    fsend, frecv, fsum, fz, fresh, obo, rbo, obs, rbs, sto, macc, mo, yb, mb, zb, fin,
    lsem, ss, rs, slot_rs,
):
    me = lax.axis_index("replica")
    t = lax.axis_index("tensor")
    y, z = t // NZ, t % NZ

    def near(o=0, yo=0, zo=0):
        return ((me + o) % NR, ((y + yo) % NY) * NZ + (z + zo) % NZ)

    zorder = (4, 3, 5, 2, 6, 1, 7)

    pairs = (
        (q_hbm, q_ref), (plan_hbm, plan), (h_hbm, h_ref), (w_hbm, w),
        (pool_hbm, pool), (table_hbm, table), (lengths_hbm, lengths),
    )
    copies = [pltpu.make_async_copy(src, dst, lsem.at[i]) for i, (src, dst) in enumerate(pairs)]
    q_copy, plan_copy, h_copy, w_copy, pool_copy, table_copy, lengths_copy = copies
    for copy in copies:
        copy.start()

    barrier = pltpu.get_barrier_semaphore()
    peers = [near(zo=o) for o in zorder] + [near(yo=o) for o in range(1, NY)]
    peers += [near(o, yo) for o in range(1, NR) for yo in range(NY)]
    for peer in peers:
        pl.semaphore_signal(barrier, inc=1, device_id=peer, device_id_type=MESH)

    q_copy.wait()
    for s in range(2):
        for j in range(4):
            qt[pl.ds(s * 4 + j, ROWS_ALL, stride=8), :] = q_ref[:, s, j * HD:(j + 1) * HD].astype(F32)
    qt[56:64] = jnp.zeros((8, HD), F32)
    qz[0] = qt[32:64].astype(BF16)
    qyz[0, 0] = qt[0:32].astype(BF16)
    qslot[NR - 1] = jnp.zeros((NY, 64, HD), BF16)
    sto[...] = jnp.zeros_like(sto)

    def push(src, dst, stage, peer, recv=None):
        pltpu.make_async_remote_copy(
            src_ref=src, dst_ref=dst, send_sem=ss.at[stage], recv_sem=rs.at[stage] if recv is None else recv,
            device_id=peer, device_id_type=MESH,
        ).start()

    def whole(ref, stage, recv=None):
        return pltpu.make_async_remote_copy(
            src_ref=ref, dst_ref=ref, send_sem=ss.at[stage], recv_sem=rs.at[stage] if recv is None else recv,
            device_id=near(1), device_id_type=MESH,
        )

    QZ, QY, QYZ, QX, FY, FZ, OZY, OY, OX, OZ = range(10)

    pl.semaphore_wait(barrier, len(peers))

    for o in zorder:
        push(qz.at[0], qz.at[o], QZ, near(zo=o))
    for yo in range(1, NY):
        push(qyz.at[0, 0], qyz.at[0, yo], QY, near(yo=yo))

    w_copy.wait()
    h_copy.wait()
    gap = jnp.zeros((1, 512), F32)
    hidden = jnp.concatenate([h_ref[:, 0].astype(F32), gap, h_ref[:, 1].astype(F32), gap], axis=0).astype(BF16)
    for kind in range(2):
        for k in range(0, KVH, 2):
            first = (kind * KVH + k) * HD
            part = jnp.dot(hidden, w[:, first:first + 2 * HD], preferred_element_type=F32)
            fsend[k // 2, 0, kind] = part[:, :HD]
            fsend[k // 2, 1, kind] = part[:, HD:]
    for yo in range(1, NY):
        push(fsend.at[(y + yo) % NY], frecv.at[yo - 1], FY, near(yo=yo))

    plan_copy.wait()
    whole(qz.at[1:NZ], QZ).wait_recv()
    chunks = [qz[(z - c + NZ) % NZ].astype(F32) for c in range(NZ)]

    def by_row(r):
        return jnp.concatenate([chunk[r * 8:(r + 1) * 8] for chunk in chunks], axis=0)

    leaving = [by_row(e) for e in range(STEAL_IN)]
    for o in range(1, NR):
        source = (me - o + NR) % NR
        chosen = jnp.zeros((64, HD), F32)
        for e in range(STEAL_IN):
            chosen = chosen + jnp.where(plan[e, 0, me] == source, leaving[e], 0.0)
        qsend[o - 1] = chosen.astype(BF16)
        for yo in range(NY):
            push(qsend.at[o - 1], qslot.at[o - 1, yo], QX, near(-o + NR, yo), slot_rs.at[(o - 1) // 2])

    whole(qyz.at[0, 1:NY], QY).wait_recv()
    for o in zorder:
        push(qyz.at[0], qyz.at[o], QYZ, near(zo=o))
    whole(frecv, FY).wait_recv()
    for c in range(2):
        for kind in range(2):
            fsum[c, kind] = fsend[y, c, kind] + frecv[0, c, kind] + frecv[1, c, kind] + frecv[2, c, kind]
    for o in zorder:
        push(fsum.at[((z + o) % NZ) // 4], fz.at[o - 1], FZ, near(zo=o))

    row_id = lax.broadcasted_iota(jnp.int32, (HD, HD), 0)
    both = jnp.bitwise_and(row_id, lanes((HD, HD)))
    parity = jnp.zeros((HD, HD), jnp.int32)
    for bit in range(7):
        parity = parity + jnp.bitwise_and(jnp.right_shift(both, bit), 1)
    signs = (1.0 - 2.0 * jnp.bitwise_and(parity, 1).astype(F32)).astype(BF16)

    pool_copy.wait()
    table_copy.wait()
    lengths_copy.wait()

    def round_trip(slot, carry):
        page = pool[slot]
        rows = jnp.concatenate([page[:, i * HD:(i + 1) * HD] for i in range(2 * KVH)], axis=0)
        turned = jnp.dot(rows, signs, preferred_element_type=F32) * INV
        scales = (jnp.max(jnp.abs(turned), axis=1, keepdims=True) + 1e-06).astype(BF16).astype(F32)
        packed = (turned * (1.0 / scales)).astype(BF16)
        back = (jnp.dot(packed, signs, preferred_element_type=F32) * (scales * INV)).astype(BF16)
        for i in range(2 * KVH):
            moved[slot, :, i * HD:(i + 1) * HD] = back[i * PAGE:(i + 1) * PAGE]
        return carry

    lax.fori_loop(0, SLOTS, round_trip, 0, unroll=4)

    lane64 = lanes((64, HD))
    row64 = lax.broadcasted_iota(jnp.int32, (64, HD), 0)
    upper = row64 < 32
    place = ((lane64 // PAGE) * NT + t) * PAGE + lane64 % PAGE
    blank = jnp.zeros((32, HD), BF16)

    def attend(pages, a, b, query, finish):
        (slots_a, span_a), (slots_b, span_b) = a, b
        valid = place < jnp.where(upper, span_a, span_b)

        def tokens(slots, first):
            return jnp.concatenate([pages[slot, :, first:first + HD] for slot in slots], axis=0)

        def spread(first, second):
            return jnp.concatenate(
                [jnp.concatenate([first, blank], axis=1), jnp.concatenate([blank, second], axis=1)], axis=0
            )

        scores, tops, lights, totals, mixed = [], [], [], [], []
        for k in range(KVH):
            wide = spread(query(0, k), query(1, k))
            keys = jnp.concatenate([tokens(slots_a, k * HD), tokens(slots_b, k * HD)], axis=1)
            scores.append(lax.dot_general(wide, keys, (((1,), (1,)), ((), ())), preferred_element_type=F32))
        for k in range(KVH):
            scores[k] = jnp.where(valid, scores[k] * INV, MASKED)
            tops.append(halves(jnp.max(scores[k], axis=1, keepdims=True)))
        for k in range(KVH):
            weights = jnp.where(valid, jnp.exp(scores[k] - (tops[k][0] + tops[k][1])), 0.0)
            totals.append(halves(jnp.sum(weights, axis=1, keepdims=True)))
            lights.append(weights.astype(BF16))
        for k in range(KVH):
            wide = spread(lights[k][:32], lights[k][32:])
            values = jnp.concatenate(
                [tokens(slots_a, (KVH + k) * HD), tokens(slots_b, (KVH + k) * HD)], axis=0
            )
            mixed.append(jnp.dot(wide, values, preferred_element_type=F32))
        finish(mixed, [top + total for top, total in zip(tops, totals)])

    def stamp(tile, pieces, first):
        for i, piece in enumerate(pieces):
            tile = jnp.where(lane64 == first + i, piece, tile)
        return tile

    def pages_of(request):
        return [table[request, j] for j in range(PPD)], lengths[request, me]

    def own_pair(p, carry):
        def finish(mixed, pieces):
            at = pl.multiple_of(p * 16, 16)
            for k in range(KVH):
                for j in range(4):
                    tile = jnp.concatenate([mixed[k][j * 8:j * 8 + 8], mixed[k][32 + j * 8:40 + j * 8]], axis=0)
                    obo[k % 2 * 4 + j, pl.ds(k // 2 * 32 + at, 16), :] = tile.astype(BF16)
            for half in range(2):
                tile = jnp.zeros((64, HD), F32)
                for k in range(half, KVH, 2):
                    tile = stamp(tile, pieces[k], (k // 2 * 2 + p) * 4)
                for j in range(4):
                    both = jnp.concatenate([tile[j * 8:j * 8 + 8], tile[32 + j * 8:40 + j * 8]], axis=0)
                    sto[half * 4 + j] = sto[half * 4 + j] + both

        def query(i, k):
            return qown[2 * p + i, k * 32:(k + 1) * 32, :]

        attend(pool, pages_of(2 * p), pages_of(2 * p + 1), query, finish)
        return carry

    def taken(o):
        taker = (me + o + 1) % NR
        request = jnp.int32(0)
        for e in range(STEAL_IN):
            request = request + jnp.where(plan[e, 0, taker] == me, plan[e, 1, taker], 0)
        return pages_of(request)

    def taken_pair(p):
        def finish(mixed, pieces):
            for k in range(KVH):
                for i in range(2):
                    obs[2 * p + i, k // 2, (k % 2) * 32:(k % 2 + 1) * 32, :] = mixed[k][i * 32:i * 32 + 32].astype(BF16)
            for c in range(NY):
                tile = jnp.zeros((64, HD), F32)
                for k in (2 * c, 2 * c + 1):
                    tile = stamp(tile, pieces[k], row64 % 32 // 16 * 4 + k % 2 * 8)
                for i in range(2):
                    both = tile[i * 32:i * 32 + 16] + tile[i * 32 + 16:i * 32 + 32]
                    obs[2 * p + i, c, 64:ONE, :] = both.astype(BF16)

        def query(i, k):
            return qslot[2 * p + i, (y - k // 2 + NY) % NY, (k % 2) * 32:(k % 2 + 1) * 32, :]

        attend(moved, taken(2 * p), taken(2 * p + 1), query, finish)

    for p in range(NR // 2):
        whole(qslot.at[2 * p:min(2 * p + 2, NR - 1)], QX, slot_rs.at[p]).wait_recv()
        taken_pair(p)
        for o in range(2 * p + 1, min(2 * p + 3, NR)):
            for yo in range(NY):
                push(obs.at[o - 1, (y + yo) % NY], rbs.at[o - 1, yo], OX, near(o, yo))

    whole(qyz.at[1:NZ], QYZ).wait_recv()
    for c in range(NT):
        four = qyz[(z - c % NZ + NZ) % NZ, (y - c // NZ + NY) % NY].astype(F32)
        for r in range(ROWS):
            macc[r, c * 8:(c + 1) * 8, :] = four[r * 8:(r + 1) * 8]
    for r in range(ROWS):
        qown[r] = macc[r].astype(BF16)
    lax.fori_loop(0, ROWS // 2, own_pair, 0)
    for c in range(NZ):
        obo[c, OWN - 16:OWN, :] = sto[c].astype(BF16)
    for o in zorder:
        push(obo.at[(z + o) % NZ], rbo.at[o - 1], OZY, near(zo=o))

    whole(rbs, OX).wait_recv()
    marks = [jnp.zeros((64, HD), F32) for _ in range(2)]
    taken_acc = []
    for e in range(STEAL_IN):
        o = jnp.minimum((me - plan[e, 0, me] + 2 * NR - 1) % NR, NR - 2)
        acc, top, total = merged([rbs[o, i] for i in range(NY)], 64)
        taken_acc.append(acc)
        marks[e % 2] = stamp(marks[e % 2], halves(top) + halves(total), e // 2 * 4)
    for c in range(NZ):
        rows = slice(c * 8, (c + 1) * 8)
        mb[c, 0:32, :] = jnp.concatenate([acc[rows] for acc in taken_acc] + [jnp.zeros((8, HD), F32)], axis=0).astype(BF16)
        mb[c, 32:LAST, :] = jnp.concatenate([mark[rows] for mark in marks], axis=0).astype(BF16)
    for o in zorder:
        push(mb.at[(z + o) % NZ], zb.at[o - 1], OZ, near(zo=o))

    whole(rbo, OZY).wait_recv()
    acc, top, total = merged([obo[z]] + [rbo[i] for i in range(NZ - 1)], NY * 32)
    pieces = halves(top) + halves(total)
    lane16 = lanes((16, HD))
    for c in range(NY):
        mo[c, 0:32, :] = acc[c * 32:(c + 1) * 32].astype(BF16)
        tile = jnp.zeros((16, HD), F32)
        for p in range(2):
            for i, piece in enumerate(pieces):
                tile = jnp.where(lane16 == p * 4 + i, piece[c * 32 + p * 16:c * 32 + p * 16 + 16], tile)
        mo[c, 32:LAST, :] = tile.astype(BF16)
    for yo in range(1, NY):
        push(mo.at[(y + yo) % NY], yb.at[yo - 1], OY, near(yo=yo))

    whole(fz, FZ).wait_recv()
    for kind in range(2):
        acc = fsum[z // 4, kind]
        for o in range(1, NZ):
            acc = acc + fz[o - 1, kind]
        fresh[kind] = acc.astype(BF16).astype(F32)

    def new_rows(kind, s):
        return jnp.concatenate(
            [jnp.broadcast_to(fresh[kind, s * 8 + r:s * 8 + r + 1, :], (8, HD)) for r in range(8)], axis=0
        )

    late = lax.broadcasted_iota(jnp.int32, (64, 1), 0) % 8 >= 4
    query = qt[...]
    tail = [jnp.sum(query * new_rows(0, s), axis=1, keepdims=True) * INV for s in range(2)]
    tail[1] = jnp.where(late, tail[1], MASKED)
    tail_top = jnp.maximum(tail[0], tail[1])

    whole(yb, OY).wait_recv()
    own = merged([mo[y]] + [yb[i] for i in range(NY - 1)], 32)
    whole(zb, OZ).wait_recv()
    others = merged([mb[z]] + [zb[i] for i in range(NZ - 1)], 32)
    acc, top, total = [jnp.concatenate(both, axis=0) for both in zip(own, others)]
    peak = jnp.maximum(top, tail_top)
    factor = jnp.exp(top - peak)
    first = jnp.exp(tail[0] - peak)
    second = jnp.where(late, jnp.exp(tail[1] - peak), 0.0)
    total = total * factor + first + second
    acc = acc * factor
    acc = acc + first.astype(BF16).astype(F32) * new_rows(1, 0)
    acc = acc + second.astype(BF16).astype(F32) * new_rows(1, 1)
    fin[...] = acc / total
    for s in range(2):
        for j in range(4):
            out_ref[:, s, j * HD:(j + 1) * HD] = fin[pl.ds(s * 4 + j, ROWS_ALL, stride=8), :].astype(BF16)

    whole(qz.at[1:NZ], QZ).wait_send()
    whole(qyz.at[0, 1:NY], QY).wait_send()
    whole(qyz.at[1:NZ], QYZ).wait_send()
    whole(frecv, FY).wait_send()
    whole(qslot.at[0:NR - 1], QX).wait_send()
    whole(fz, FZ).wait_send()
    whole(rbo, OZY).wait_send()
    whole(rbs, OX).wait_send()
    whole(yb, OY).wait_send()
    whole(zb, OZ).wait_send()


def on_device(kv_pool, page_table, lengths, steal_plan, hidden_rows, kv_weight, queries):
    hbm = pl.BlockSpec(memory_space=pltpu.HBM)
    width = 2 * KVH * HD

    def half(*shape):
        return pltpu.VMEM((*shape, HD), BF16)

    def full(*shape):
        return pltpu.VMEM((*shape, HD), F32)

    out = pl.pallas_call(
        kernel,
        out_shape=jax.ShapeDtypeStruct((ROWS_ALL, 2, 512), BF16),
        in_specs=[hbm] * 7,
        out_specs=pl.BlockSpec(memory_space=pltpu.VMEM),
        scratch_shapes=[
            pltpu.SMEM((ROWS, PPD), jnp.int32),
            pltpu.SMEM((ROWS, NR), jnp.int32),
            pltpu.SMEM((STEAL_IN, 2, NR), jnp.int32),
            pltpu.VMEM((ROWS_ALL, 2, 512), BF16),
            pltpu.VMEM((ROWS_ALL, 2, 512), BF16),
            pltpu.VMEM((SLOTS, PAGE, width), BF16),
            pltpu.VMEM((SLOTS, PAGE, width), BF16),
            pltpu.VMEM((512, width), BF16),
            full(64), half(NZ, 32), half(NZ, NY, 32), half(ROWS, 256), half(NR - 1, 64), half(NR, NY, 64),
            full(NY, 2, 2, 16), full(NY - 1, 2, 2, 16), full(2, 2, 16), full(NZ - 1, 2, 16), full(2, 16),
            half(NZ, OWN), half(NZ - 1, OWN), half(NR, NY, ONE), half(NR - 1, NY, ONE),
            full(NZ, 16), full(ROWS, 256), half(NY, LAST), half(NY - 1, LAST), half(NZ, LAST), half(NZ - 1, LAST),
            full(64),
            pltpu.SemaphoreType.DMA((7,)),
            pltpu.SemaphoreType.DMA((10,)),
            pltpu.SemaphoreType.DMA((10,)),
            pltpu.SemaphoreType.DMA((NR // 2,)),
        ],
        compiler_params=pltpu.CompilerParams(
            collective_id=0, has_side_effects=True, vmem_limit_bytes=63 * 2**20
        ),
    )(
        page_table[0], lengths.T, steal_plan.transpose(1, 2, 0), queries[0].transpose(1, 0, 2),
        hidden_rows[0].transpose(1, 0, 2), kv_pool[0], kv_weight,
    )
    return out.transpose(1, 0, 2)[None]


def solution(mesh):
    return jax.shard_map(
        on_device,
        mesh=mesh,
        in_specs=(
            P("replica", "tensor", None, None),
            P("replica", None, "tensor"),
            P(),
            P(),
            P("replica", None, None, "tensor"),
            P("tensor", None),
            P("replica", None, None, "tensor"),
        ),
        out_specs=P("replica", None, None, "tensor"),
        check_vma=False,
    )
```

```python
import functools
import math

import jax
import jax.numpy as jnp
from jax import lax
from jax.experimental import pallas as pl
from jax.experimental.pallas import tpu as pltpu
from jax.sharding import PartitionSpec as P

KVH = 8
HD = 128
PAGE = 32
PPD = 4
STEAL_IN = 3
ROWS = 4
ROWS_ALL = 7
SLOTS = 16
NR = 8
NY = 4
NZ = 8
NT = NY * NZ
MASKED = -1e30
MESH = pl.DeviceIdType.MESH
F32 = jnp.float32
BF16 = jnp.bfloat16
INV = 1.0 / math.sqrt(HD)
OWN = NY * ROWS * 8 + 16
LAST = 32 + 16


def lanes(shape):
    return lax.broadcasted_iota(jnp.int32, shape, len(shape) - 1)


def halves(x):
    high = x.astype(BF16).astype(F32)
    return high, (x - high).astype(BF16).astype(F32)


def stat_factors(tiles):
    tops = [tile + pltpu.roll(tile, 127, 1) for tile in tiles]
    totals = [pltpu.roll(one, 126, 1) for one in tops]
    top = functools.reduce(jnp.maximum, tops)
    factors = [jnp.exp(one - top) for one in tops]
    total = sum(f * l for f, l in zip(factors, totals))
    return top, total, factors


def column(x, groups):
    return jnp.concatenate([x[:, 4 * g:4 * g + 1] for g in range(groups)], axis=0)


def merged(held, rows):
    groups = rows // 16
    top, total, factors = stat_factors([part[rows:rows + 16].astype(F32) for part in held])
    acc = sum(column(f, groups) * part[:rows].astype(F32) for f, part in zip(factors, held))
    return acc, column(top, groups), column(total, groups)


def kernel(
    table_hbm, lengths_hbm, plan_hbm, q_hbm, h_hbm, pool_hbm, w_hbm, out_ref,
    table, lengths, plan, q_ref, h_ref, pool, moved, w, qt, qz, qyz, qown, qsend, qslot,
    fsend, frecv, fsum, fz, fresh, obo, rbo, obs, rbs, ost, rst, sto, macc, mo, yb, mb, zb, fin,
    lsem, ss, rs, slot_rs,
):
    me = lax.axis_index("replica")
    t = lax.axis_index("tensor")
    y, z = t // NZ, t % NZ

    def near(o=0, yo=0, zo=0):
        return ((me + o) % NR, ((y + yo) % NY) * NZ + (z + zo) % NZ)

    zorder = (4, 3, 5, 2, 6, 1, 7)

    pairs = (
        (q_hbm, q_ref), (plan_hbm, plan), (h_hbm, h_ref), (w_hbm, w),
        (pool_hbm, pool), (table_hbm, table), (lengths_hbm, lengths),
    )
    copies = [pltpu.make_async_copy(src, dst, lsem.at[i]) for i, (src, dst) in enumerate(pairs)]
    q_copy, plan_copy, h_copy, w_copy, pool_copy, table_copy, lengths_copy = copies
    for copy in copies:
        copy.start()

    barrier = pltpu.get_barrier_semaphore()
    peers = [near(zo=o) for o in zorder] + [near(yo=o) for o in range(1, NY)]
    peers += [near(o, yo) for o in range(1, NR) for yo in range(NY)]
    for peer in peers:
        pl.semaphore_signal(barrier, inc=1, device_id=peer, device_id_type=MESH)

    q_copy.wait()
    for s in range(2):
        for j in range(4):
            qt[pl.ds(s * 4 + j, ROWS_ALL, stride=8), :] = q_ref[:, s, j * HD:(j + 1) * HD].astype(F32)
    qt[56:64] = jnp.zeros((8, HD), F32)
    qz[0] = qt[32:64].astype(BF16)
    qyz[0, 0] = qt[0:32].astype(BF16)
    qslot[NR - 1] = jnp.zeros((NY, 64, HD), BF16)
    sto[...] = jnp.zeros_like(sto)

    def push(src, dst, stage, peer, recv=None):
        pltpu.make_async_remote_copy(
            src_ref=src, dst_ref=dst, send_sem=ss.at[stage], recv_sem=rs.at[stage] if recv is None else recv,
            device_id=peer, device_id_type=MESH,
        ).start()

    def whole(ref, stage, recv=None):
        return pltpu.make_async_remote_copy(
            src_ref=ref, dst_ref=ref, send_sem=ss.at[stage], recv_sem=rs.at[stage] if recv is None else recv,
            device_id=near(1), device_id_type=MESH,
        )

    QZ, QY, QYZ, QX, FY, FZ, OZY, OY, OX, OS, OZ = range(11)

    pl.semaphore_wait(barrier, len(peers))

    for o in zorder:
        push(qz.at[0], qz.at[o], QZ, near(zo=o))
    for yo in range(1, NY):
        push(qyz.at[0, 0], qyz.at[0, yo], QY, near(yo=yo))

    w_copy.wait()
    h_copy.wait()
    gap = jnp.zeros((1, 512), F32)
    hidden = jnp.concatenate([h_ref[:, 0].astype(F32), gap, h_ref[:, 1].astype(F32), gap], axis=0).astype(BF16)
    for kind in range(2):
        for k in range(0, KVH, 2):
            first = (kind * KVH + k) * HD
            part = jnp.dot(hidden, w[:, first:first + 2 * HD], preferred_element_type=F32)
            fsend[k // 2, 0, kind] = part[:, :HD]
            fsend[k // 2, 1, kind] = part[:, HD:]
    for yo in range(1, NY):
        push(fsend.at[(y + yo) % NY], frecv.at[yo - 1], FY, near(yo=yo))

    plan_copy.wait()
    whole(qz.at[1:NZ], QZ).wait_recv()
    chunks = [qz[(z - c + NZ) % NZ].astype(F32) for c in range(NZ)]

    def by_row(r):
        return jnp.concatenate([chunk[r * 8:(r + 1) * 8] for chunk in chunks], axis=0)

    leaving = [by_row(e) for e in range(STEAL_IN)]
    for o in range(1, NR):
        source = (me - o + NR) % NR
        chosen = jnp.zeros((64, HD), F32)
        for e in range(STEAL_IN):
            chosen = chosen + jnp.where(plan[e, 0, me] == source, leaving[e], 0.0)
        qsend[o - 1] = chosen.astype(BF16)
        for yo in range(NY):
            push(qsend.at[o - 1], qslot.at[o - 1, yo], QX, near(-o + NR, yo), slot_rs.at[(o - 1) // 2])

    whole(qyz.at[0, 1:NY], QY).wait_recv()
    for o in zorder:
        push(qyz.at[0], qyz.at[o], QYZ, near(zo=o))
    whole(frecv, FY).wait_recv()
    for c in range(2):
        for kind in range(2):
            fsum[c, kind] = fsend[y, c, kind] + frecv[0, c, kind] + frecv[1, c, kind] + frecv[2, c, kind]
    for o in zorder:
        push(fsum.at[((z + o) % NZ) // 4], fz.at[o - 1], FZ, near(zo=o))

    row_id = lax.broadcasted_iota(jnp.int32, (HD, HD), 0)
    both = jnp.bitwise_and(row_id, lanes((HD, HD)))
    parity = jnp.zeros((HD, HD), jnp.int32)
    for bit in range(7):
        parity = parity + jnp.bitwise_and(jnp.right_shift(both, bit), 1)
    signs = (1.0 - 2.0 * jnp.bitwise_and(parity, 1).astype(F32)).astype(BF16)

    pool_copy.wait()
    table_copy.wait()
    lengths_copy.wait()

    def round_trip(slot, carry):
        page = pool[slot]
        rows = jnp.concatenate([page[:, i * HD:(i + 1) * HD] for i in range(2 * KVH)], axis=0)
        turned = jnp.dot(rows, signs, preferred_element_type=F32) * INV
        scales = (jnp.max(jnp.abs(turned), axis=1, keepdims=True) + 1e-06).astype(BF16).astype(F32)
        packed = (turned * (1.0 / scales)).astype(BF16)
        back = (jnp.dot(packed, signs, preferred_element_type=F32) * (scales * INV)).astype(BF16)
        for i in range(2 * KVH):
            moved[slot, :, i * HD:(i + 1) * HD] = back[i * PAGE:(i + 1) * PAGE]
        return carry

    lax.fori_loop(0, SLOTS, round_trip, 0, unroll=4)

    lane64 = lanes((64, HD))
    row64 = lax.broadcasted_iota(jnp.int32, (64, HD), 0)
    upper = row64 < 32
    place = ((lane64 // PAGE) * NT + t) * PAGE + lane64 % PAGE
    blank = jnp.zeros((32, HD), BF16)

    def attend(pages, a, b, query, finish):
        (slots_a, span_a), (slots_b, span_b) = a, b
        valid = place < jnp.where(upper, span_a, span_b)

        def tokens(slots, first):
            return jnp.concatenate([pages[slot, :, first:first + HD] for slot in slots], axis=0)

        def spread(first, second):
            return jnp.concatenate(
                [jnp.concatenate([first, blank], axis=1), jnp.concatenate([blank, second], axis=1)], axis=0
            )

        scores, tops, lights, totals, mixed = [], [], [], [], []
        for k in range(KVH):
            wide = spread(query(0, k), query(1, k))
            keys = jnp.concatenate([tokens(slots_a, k * HD), tokens(slots_b, k * HD)], axis=1)
            scores.append(lax.dot_general(wide, keys, (((1,), (1,)), ((), ())), preferred_element_type=F32))
        for k in range(KVH):
            scores[k] = jnp.where(valid, scores[k] * INV, MASKED)
            tops.append(halves(jnp.max(scores[k], axis=1, keepdims=True)))
        for k in range(KVH):
            weights = jnp.where(valid, jnp.exp(scores[k] - (tops[k][0] + tops[k][1])), 0.0)
            totals.append(halves(jnp.sum(weights, axis=1, keepdims=True)))
            lights.append(weights.astype(BF16))
        for k in range(KVH):
            wide = spread(lights[k][:32], lights[k][32:])
            values = jnp.concatenate(
                [tokens(slots_a, (KVH + k) * HD), tokens(slots_b, (KVH + k) * HD)], axis=0
            )
            mixed.append(jnp.dot(wide, values, preferred_element_type=F32))
        finish(mixed, [top + total for top, total in zip(tops, totals)])

    def stamp(tile, pieces, first):
        for i, piece in enumerate(pieces):
            tile = jnp.where(lane64 == first + i, piece, tile)
        return tile

    def pages_of(request):
        return [table[request, j] for j in range(PPD)], lengths[request, me]

    def own_pair(p, carry):
        def finish(mixed, pieces):
            at = pl.multiple_of(p * 16, 16)
            for k in range(KVH):
                for j in range(4):
                    tile = jnp.concatenate([mixed[k][j * 8:j * 8 + 8], mixed[k][32 + j * 8:40 + j * 8]], axis=0)
                    obo[k % 2 * 4 + j, pl.ds(k // 2 * 32 + at, 16), :] = tile.astype(BF16)
            for half in range(2):
                tile = jnp.zeros((64, HD), F32)
                for k in range(half, KVH, 2):
                    tile = stamp(tile, pieces[k], (k // 2 * 2 + p) * 4)
                for j in range(4):
                    both = jnp.concatenate([tile[j * 8:j * 8 + 8], tile[32 + j * 8:40 + j * 8]], axis=0)
                    sto[half * 4 + j] = sto[half * 4 + j] + both

        def query(i, k):
            return qown[2 * p + i, k * 32:(k + 1) * 32, :]

        attend(pool, pages_of(2 * p), pages_of(2 * p + 1), query, finish)
        return carry

    def taken(o):
        taker = (me + o + 1) % NR
        request = jnp.int32(0)
        for e in range(STEAL_IN):
            request = request + jnp.where(plan[e, 0, taker] == me, plan[e, 1, taker], 0)
        return pages_of(request)

    def taken_pair(p):
        def finish(mixed, pieces):
            for k in range(KVH):
                for i in range(2):
                    obs[2 * p + i, k // 2, (k % 2) * 32:(k % 2 + 1) * 32, :] = mixed[k][i * 32:i * 32 + 32].astype(BF16)
            tile = jnp.zeros((64, HD), F32)
            for k in range(KVH):
                tile = jnp.where(lane64 == k, pieces[k][0] + pieces[k][1], tile)
                tile = jnp.where(lane64 == KVH + k, pieces[k][2] + pieces[k][3], tile)
            across = jnp.concatenate([tile, jnp.zeros((64, HD), F32)], axis=0).T
            both = jnp.where(lanes((KVH, HD)) < 64, across[:KVH], pltpu.roll(across[KVH:2 * KVH], 64, 1))
            for c in range(NY):
                ost[p, c] = both[2 * c:2 * c + 2]

        def query(i, k):
            return qslot[2 * p + i, (y - k // 2 + NY) % NY, (k % 2) * 32:(k % 2 + 1) * 32, :]

        attend(moved, taken(2 * p), taken(2 * p + 1), query, finish)

    for p in range(NR // 2):
        whole(qslot.at[2 * p:min(2 * p + 2, NR - 1)], QX, slot_rs.at[p]).wait_recv()
        taken_pair(p)
        for o in range(2 * p + 1, min(2 * p + 3, NR)):
            for yo in range(NY):
                push(obs.at[o - 1, (y + yo) % NY], rbs.at[o - 1, yo], OX, near(o, yo))
                push(ost.at[p, (y + yo) % NY], rst.at[o - 1, yo], OS, near(o, yo))

    whole(qyz.at[1:NZ], QYZ).wait_recv()
    for c in range(NT):
        four = qyz[(z - c % NZ + NZ) % NZ, (y - c // NZ + NY) % NY].astype(F32)
        for r in range(ROWS):
            macc[r, c * 8:(c + 1) * 8, :] = four[r * 8:(r + 1) * 8]
    for r in range(ROWS):
        qown[r] = macc[r].astype(BF16)
    lax.fori_loop(0, ROWS // 2, own_pair, 0)
    for c in range(NZ):
        obo[c, OWN - 16:OWN, :] = sto[c].astype(BF16)
    for o in zorder:
        push(obo.at[(z + o) % NZ], rbo.at[o - 1], OZY, near(zo=o))

    whole(rst, OS).wait_recv()
    index = [jnp.minimum((me - plan[e, 0, me] + 2 * NR - 1) % NR, NR - 2) for e in range(STEAL_IN)]
    row8 = lax.broadcasted_iota(jnp.int32, (8, HD), 0) // 2
    second = jnp.zeros((8, HD), jnp.int32)
    for e in range(STEAL_IN):
        second = jnp.where(row8 == e, index[e] % 2, second)
    tops = []
    for i in range(NY):
        tile = jnp.concatenate([rst[index[e], i] for e in range(STEAL_IN)] + [jnp.zeros((2, HD), F32)], axis=0)
        tops.append(jnp.where(second == 1, pltpu.roll(tile, 96, 1), tile))
    top = functools.reduce(jnp.maximum, tops)
    factors = [jnp.exp(one - top) for one in tops]
    total = sum(f * pltpu.roll(one, 64, 1) for f, one in zip(factors, tops))
    down = jnp.concatenate(factors + [top, total, jnp.zeros((HD - 48, HD), F32)], axis=0).T

    def down_column(i, e):
        first = i * 8 + 2 * e
        return jnp.concatenate([down[:32, first:first + 1], down[:32, first + 1:first + 2]], axis=0)

    whole(rbs, OX).wait_recv()
    marks = [jnp.zeros((64, HD), F32) for _ in range(2)]
    taken_acc = []
    for e in range(STEAL_IN):
        taken_acc.append(sum(down_column(i, e) * rbs[index[e], i].astype(F32) for i in range(NY)))
        marks[e % 2] = stamp(marks[e % 2], halves(down_column(NY, e)) + halves(down_column(NY + 1, e)), e // 2 * 4)
    for c in range(NZ):
        rows = slice(c * 8, (c + 1) * 8)
        mb[c, 0:32, :] = jnp.concatenate([acc[rows] for acc in taken_acc] + [jnp.zeros((8, HD), F32)], axis=0).astype(BF16)
        mb[c, 32:LAST, :] = jnp.concatenate([mark[rows] for mark in marks], axis=0).astype(BF16)
    for o in zorder:
        push(mb.at[(z + o) % NZ], zb.at[o - 1], OZ, near(zo=o))

    whole(rbo, OZY).wait_recv()
    acc, top, total = merged([obo[z]] + [rbo[i] for i in range(NZ - 1)], NY * 32)
    pieces = halves(top) + halves(total)
    lane16 = lanes((16, HD))
    for c in range(NY):
        mo[c, 0:32, :] = acc[c * 32:(c + 1) * 32].astype(BF16)
        tile = jnp.zeros((16, HD), F32)
        for p in range(2):
            for i, piece in enumerate(pieces):
                tile = jnp.where(lane16 == p * 4 + i, piece[c * 32 + p * 16:c * 32 + p * 16 + 16], tile)
        mo[c, 32:LAST, :] = tile.astype(BF16)
    for yo in range(1, NY):
        push(mo.at[(y + yo) % NY], yb.at[yo - 1], OY, near(yo=yo))

    whole(fz, FZ).wait_recv()
    for kind in range(2):
        acc = fsum[z // 4, kind]
        for o in range(1, NZ):
            acc = acc + fz[o - 1, kind]
        fresh[kind] = acc.astype(BF16).astype(F32)

    def new_rows(kind, s):
        return jnp.concatenate(
            [jnp.broadcast_to(fresh[kind, s * 8 + r:s * 8 + r + 1, :], (8, HD)) for r in range(8)], axis=0
        )

    late = lax.broadcasted_iota(jnp.int32, (64, 1), 0) % 8 >= 4
    query = qt[...]
    tail = [jnp.sum(query * new_rows(0, s), axis=1, keepdims=True) * INV for s in range(2)]
    tail[1] = jnp.where(late, tail[1], MASKED)
    tail_top = jnp.maximum(tail[0], tail[1])

    whole(yb, OY).wait_recv()
    own = merged([mo[y]] + [yb[i] for i in range(NY - 1)], 32)
    whole(zb, OZ).wait_recv()
    others = merged([mb[z]] + [zb[i] for i in range(NZ - 1)], 32)
    acc, top, total = [jnp.concatenate(both, axis=0) for both in zip(own, others)]
    peak = jnp.maximum(top, tail_top)
    factor = jnp.exp(top - peak)
    first = jnp.exp(tail[0] - peak)
    second = jnp.where(late, jnp.exp(tail[1] - peak), 0.0)
    total = total * factor + first + second
    acc = acc * factor
    acc = acc + first.astype(BF16).astype(F32) * new_rows(1, 0)
    acc = acc + second.astype(BF16).astype(F32) * new_rows(1, 1)
    fin[...] = acc / total
    for s in range(2):
        for j in range(4):
            out_ref[:, s, j * HD:(j + 1) * HD] = fin[pl.ds(s * 4 + j, ROWS_ALL, stride=8), :].astype(BF16)

    whole(qz.at[1:NZ], QZ).wait_send()
    whole(qyz.at[0, 1:NY], QY).wait_send()
    whole(qyz.at[1:NZ], QYZ).wait_send()
    whole(frecv, FY).wait_send()
    whole(qslot.at[0:NR - 1], QX).wait_send()
    whole(fz, FZ).wait_send()
    whole(rbo, OZY).wait_send()
    whole(rbs, OX).wait_send()
    whole(rst, OS).wait_send()
    whole(yb, OY).wait_send()
    whole(zb, OZ).wait_send()


def on_device(kv_pool, page_table, lengths, steal_plan, hidden_rows, kv_weight, queries):
    hbm = pl.BlockSpec(memory_space=pltpu.HBM)
    width = 2 * KVH * HD

    def half(*shape):
        return pltpu.VMEM((*shape, HD), BF16)

    def full(*shape):
        return pltpu.VMEM((*shape, HD), F32)

    out = pl.pallas_call(
        kernel,
        out_shape=pltpu.VMEM((ROWS_ALL, 2, 512), BF16),
        in_specs=[hbm] * 7,
        out_specs=pl.BlockSpec(memory_space=pltpu.VMEM),
        scratch_shapes=[
            pltpu.SMEM((ROWS, PPD), jnp.int32),
            pltpu.SMEM((ROWS, NR), jnp.int32),
            pltpu.SMEM((STEAL_IN, 2, NR), jnp.int32),
            pltpu.VMEM((ROWS_ALL, 2, 512), BF16),
            pltpu.VMEM((ROWS_ALL, 2, 512), BF16),
            pltpu.VMEM((SLOTS, PAGE, width), BF16),
            pltpu.VMEM((SLOTS, PAGE, width), BF16),
            pltpu.VMEM((512, width), BF16),
            full(64), half(NZ, 32), half(NZ, NY, 32), half(ROWS, 256), half(NR - 1, 64), half(NR, NY, 64),
            full(NY, 2, 2, 16), full(NY - 1, 2, 2, 16), full(2, 2, 16), full(NZ - 1, 2, 16), full(2, 16),
            half(NZ, OWN), half(NZ - 1, OWN), half(NR, NY, 64), half(NR - 1, NY, 64), full(NR // 2, NY, 2), full(NR - 1, NY, 2),
            full(NZ, 16), full(ROWS, 256), half(NY, LAST), half(NY - 1, LAST), half(NZ, LAST), half(NZ - 1, LAST),
            full(64),
            pltpu.SemaphoreType.DMA((7,)),
            pltpu.SemaphoreType.DMA((11,)),
            pltpu.SemaphoreType.DMA((11,)),
            pltpu.SemaphoreType.DMA((NR // 2,)),
        ],
        compiler_params=pltpu.CompilerParams(
            collective_id=0, has_side_effects=True, vmem_limit_bytes=63 * 2**20
        ),
    )(
        page_table[0], lengths.T, steal_plan.transpose(1, 2, 0), queries[0].transpose(1, 0, 2),
        hidden_rows[0].transpose(1, 0, 2), kv_pool[0], kv_weight,
    )
    return out.transpose(1, 0, 2)[None]


def solution(mesh):
    return jax.shard_map(
        on_device,
        mesh=mesh,
        in_specs=(
            P("replica", "tensor", None, None),
            P("replica", None, "tensor"),
            P(),
            P(),
            P("replica", None, None, "tensor"),
            P("tensor", None),
            P("replica", None, None, "tensor"),
        ),
        out_specs=P("replica", None, None, "tensor"),
        check_vma=False,
    )
```

```python
import functools
import math

import jax
import jax.numpy as jnp
from jax import lax
from jax.experimental import pallas as pl
from jax.experimental.pallas import tpu as pltpu
from jax.sharding import PartitionSpec as P

KVH = 8
HD = 128
PAGE = 32
PPD = 4
STEAL_IN = 3
ROWS = 4
ROWS_ALL = 7
SLOTS = 16
NR = 8
NY = 4
NZ = 8
NT = NY * NZ
MASKED = -1e30
MESH = pl.DeviceIdType.MESH
F32 = jnp.float32
BF16 = jnp.bfloat16
INV = 1.0 / math.sqrt(HD)
OWN = NY * ROWS * 8 + 16
LAST = 32 + 16


def lanes(shape):
    return lax.broadcasted_iota(jnp.int32, shape, len(shape) - 1)


def halves(x):
    high = x.astype(BF16).astype(F32)
    return high, (x - high).astype(BF16).astype(F32)


def stat_factors(tiles):
    tops = [tile + pltpu.roll(tile, 127, 1) for tile in tiles]
    totals = [pltpu.roll(one, 126, 1) for one in tops]
    top = functools.reduce(jnp.maximum, tops)
    factors = [jnp.exp(one - top) for one in tops]
    total = sum(f * l for f, l in zip(factors, totals))
    return top, total, factors


def column(x, groups):
    return jnp.concatenate([x[:, 4 * g:4 * g + 1] for g in range(groups)], axis=0)


def merged(held, rows):
    groups = rows // 16
    top, total, factors = stat_factors([part[rows:rows + 16].astype(F32) for part in held])
    acc = sum(column(f, groups) * part[:rows].astype(F32) for f, part in zip(factors, held))
    return acc, column(top, groups), column(total, groups)


def kernel(
    table_hbm, lengths_hbm, plan_hbm, q_hbm, h_hbm, pool_hbm, w_hbm, out_ref,
    table, lengths, plan, q_ref, h_ref, pool, moved, w, qt, qz, qyz, qown, qsend, qslot,
    fsend, frecv, fsum, fz, fresh, obo, rbo, obs, rbs, ost, rst, sto, macc, mo, yb, mb, zb, fin,
    lsem, ss, rs, slot_rs,
):
    me = lax.axis_index("replica")
    t = lax.axis_index("tensor")
    y, z = t // NZ, t % NZ

    def near(o=0, yo=0, zo=0):
        return ((me + o) % NR, ((y + yo) % NY) * NZ + (z + zo) % NZ)

    zorder = (4, 3, 5, 2, 6, 1, 7)

    pairs = (
        (q_hbm, q_ref), (plan_hbm, plan), (h_hbm, h_ref), (w_hbm, w),
        (pool_hbm, pool), (table_hbm, table), (lengths_hbm, lengths),
    )
    copies = [pltpu.make_async_copy(src, dst, lsem.at[i]) for i, (src, dst) in enumerate(pairs)]
    q_copy, plan_copy, h_copy, w_copy, pool_copy, table_copy, lengths_copy = copies
    for copy in copies:
        copy.start()

    barrier = pltpu.get_barrier_semaphore()
    peers = [near(zo=o) for o in zorder] + [near(yo=o) for o in range(1, NY)]
    peers += [near(o, yo) for o in range(1, NR) for yo in range(NY)]
    for peer in peers:
        pl.semaphore_signal(barrier, inc=1, device_id=peer, device_id_type=MESH)

    q_copy.wait()
    for s in range(2):
        for j in range(4):
            qt[pl.ds(s * 4 + j, ROWS_ALL, stride=8), :] = q_ref[:, s, j * HD:(j + 1) * HD].astype(F32)
    qt[56:64] = jnp.zeros((8, HD), F32)
    qz[0] = qt[32:64].astype(BF16)
    qyz[0, 0] = qt[0:32].astype(BF16)
    qslot[NR - 1] = jnp.zeros((NY, 64, HD), BF16)
    sto[...] = jnp.zeros_like(sto)

    def push(src, dst, stage, peer, recv=None):
        pltpu.make_async_remote_copy(
            src_ref=src, dst_ref=dst, send_sem=ss.at[stage], recv_sem=rs.at[stage] if recv is None else recv,
            device_id=peer, device_id_type=MESH,
        ).start()

    def whole(ref, stage, recv=None):
        return pltpu.make_async_remote_copy(
            src_ref=ref, dst_ref=ref, send_sem=ss.at[stage], recv_sem=rs.at[stage] if recv is None else recv,
            device_id=near(1), device_id_type=MESH,
        )

    QZ, QY, QYZ, QX, FY, FZ, OZY, OY, OX, OS, OZ = range(11)

    pl.semaphore_wait(barrier, len(peers))

    for o in zorder:
        push(qz.at[0], qz.at[o], QZ, near(zo=o))
    for yo in range(1, NY):
        push(qyz.at[0, 0], qyz.at[0, yo], QY, near(yo=yo))

    w_copy.wait()
    h_copy.wait()
    gap = jnp.zeros((1, 512), F32)
    hidden = jnp.concatenate([h_ref[:, 0].astype(F32), gap, h_ref[:, 1].astype(F32), gap], axis=0).astype(BF16)
    for kind in range(2):
        for k in range(0, KVH, 2):
            first = (kind * KVH + k) * HD
            part = jnp.dot(hidden, w[:, first:first + 2 * HD], preferred_element_type=F32)
            fsend[k // 2, 0, kind] = part[:, :HD]
            fsend[k // 2, 1, kind] = part[:, HD:]
    for yo in range(1, NY):
        push(fsend.at[(y + yo) % NY], frecv.at[yo - 1], FY, near(yo=yo))

    plan_copy.wait()
    whole(qz.at[1:NZ], QZ).wait_recv()
    chunks = [qz[(z - c + NZ) % NZ].astype(F32) for c in range(NZ)]

    def by_row(r):
        return jnp.concatenate([chunk[r * 8:(r + 1) * 8] for chunk in chunks], axis=0)

    leaving = [by_row(e) for e in range(STEAL_IN)]
    for o in range(1, NR):
        source = (me - o + NR) % NR
        chosen = jnp.zeros((64, HD), F32)
        for e in range(STEAL_IN):
            chosen = chosen + jnp.where(plan[e, 0, me] == source, leaving[e], 0.0)
        qsend[o - 1] = chosen.astype(BF16)
        for yo in range(NY):
            push(qsend.at[o - 1], qslot.at[o - 1, yo], QX, near(-o + NR, yo), slot_rs.at[(o - 1) // 2])

    whole(qyz.at[0, 1:NY], QY).wait_recv()
    for o in zorder:
        push(qyz.at[0], qyz.at[o], QYZ, near(zo=o))
    whole(frecv, FY).wait_recv()
    for c in range(2):
        for kind in range(2):
            fsum[c, kind] = fsend[y, c, kind] + frecv[0, c, kind] + frecv[1, c, kind] + frecv[2, c, kind]
    for o in zorder:
        push(fsum.at[((z + o) % NZ) // 4], fz.at[o - 1], FZ, near(zo=o))

    row_id = lax.broadcasted_iota(jnp.int32, (HD, HD), 0)
    both = jnp.bitwise_and(row_id, lanes((HD, HD)))
    parity = jnp.zeros((HD, HD), jnp.int32)
    for bit in range(7):
        parity = parity + jnp.bitwise_and(jnp.right_shift(both, bit), 1)
    signs = (1.0 - 2.0 * jnp.bitwise_and(parity, 1).astype(F32)).astype(BF16)

    pool_copy.wait()
    table_copy.wait()
    lengths_copy.wait()

    def round_trip(slot, carry):
        page = pool[slot]
        rows = jnp.concatenate([page[:, i * HD:(i + 1) * HD] for i in range(2 * KVH)], axis=0)
        turned = jnp.dot(rows, signs, preferred_element_type=F32) * INV
        scales = (jnp.max(jnp.abs(turned), axis=1, keepdims=True) + 1e-06).astype(BF16).astype(F32)
        packed = (turned * (1.0 / scales)).astype(BF16)
        back = (jnp.dot(packed, signs, preferred_element_type=F32) * (scales * INV)).astype(BF16)
        for i in range(2 * KVH):
            moved[slot, :, i * HD:(i + 1) * HD] = back[i * PAGE:(i + 1) * PAGE]
        return carry

    lax.fori_loop(0, SLOTS, round_trip, 0, unroll=4)

    lane64 = lanes((64, HD))
    row64 = lax.broadcasted_iota(jnp.int32, (64, HD), 0)
    upper = row64 < 32
    place = ((lane64 // PAGE) * NT + t) * PAGE + lane64 % PAGE
    blank = jnp.zeros((32, HD), BF16)

    def attend(pages, a, b, query, finish):
        (slots_a, span_a), (slots_b, span_b) = a, b
        valid = place < jnp.where(upper, span_a, span_b)

        def tokens(slots, first):
            return jnp.concatenate([pages[slot, :, first:first + HD] for slot in slots], axis=0)

        def spread(first, second):
            return jnp.concatenate(
                [jnp.concatenate([first, blank], axis=1), jnp.concatenate([blank, second], axis=1)], axis=0
            )

        scores, tops, lights, totals, mixed = [], [], [], [], []
        for k in range(KVH):
            wide = spread(query(0, k), query(1, k))
            keys = jnp.concatenate([tokens(slots_a, k * HD), tokens(slots_b, k * HD)], axis=1)
            scores.append(lax.dot_general(wide, keys, (((1,), (1,)), ((), ())), preferred_element_type=F32))
        for k in range(KVH):
            scores[k] = jnp.where(valid, scores[k] * INV, MASKED)
            tops.append(halves(jnp.max(scores[k], axis=1, keepdims=True)))
        for k in range(KVH):
            weights = jnp.where(valid, jnp.exp(scores[k] - (tops[k][0] + tops[k][1])), 0.0)
            totals.append(halves(jnp.sum(weights, axis=1, keepdims=True)))
            lights.append(weights.astype(BF16))
        for k in range(KVH):
            wide = spread(lights[k][:32], lights[k][32:])
            values = jnp.concatenate(
                [tokens(slots_a, (KVH + k) * HD), tokens(slots_b, (KVH + k) * HD)], axis=0
            )
            mixed.append(jnp.dot(wide, values, preferred_element_type=F32))
        finish(mixed, [top + total for top, total in zip(tops, totals)])

    def stamp(tile, pieces, first):
        for i, piece in enumerate(pieces):
            tile = jnp.where(lane64 == first + i, piece, tile)
        return tile

    def pages_of(request):
        return [table[request, j] for j in range(PPD)], lengths[request, me]

    def own_pair(p, carry):
        def finish(mixed, pieces):
            at = pl.multiple_of(p * 16, 16)
            for k in range(KVH):
                for j in range(4):
                    tile = jnp.concatenate([mixed[k][j * 8:j * 8 + 8], mixed[k][32 + j * 8:40 + j * 8]], axis=0)
                    obo[k % 2 * 4 + j, pl.ds(k // 2 * 32 + at, 16), :] = tile.astype(BF16)
            for half in range(2):
                tile = jnp.zeros((64, HD), F32)
                for k in range(half, KVH, 2):
                    tile = stamp(tile, pieces[k], (k // 2 * 2 + p) * 4)
                for j in range(4):
                    both = jnp.concatenate([tile[j * 8:j * 8 + 8], tile[32 + j * 8:40 + j * 8]], axis=0)
                    sto[half * 4 + j] = sto[half * 4 + j] + both

        def query(i, k):
            return qown[2 * p + i, k * 32:(k + 1) * 32, :]

        attend(pool, pages_of(2 * p), pages_of(2 * p + 1), query, finish)
        return carry

    def taken(o):
        taker = (me + o + 1) % NR
        request = jnp.int32(0)
        for e in range(STEAL_IN):
            request = request + jnp.where(plan[e, 0, taker] == me, plan[e, 1, taker], 0)
        return pages_of(request)

    def taken_pair(p):
        def finish(mixed, pieces):
            for k in range(KVH):
                for i in range(2):
                    obs[2 * p + i, k // 2, (k % 2) * 32:(k % 2 + 1) * 32, :] = mixed[k][i * 32:i * 32 + 32].astype(BF16)
            tile = jnp.zeros((64, HD), F32)
            for k in range(KVH):
                tile = jnp.where(lane64 == k, pieces[k][0] + pieces[k][1], tile)
                tile = jnp.where(lane64 == KVH + k, pieces[k][2] + pieces[k][3], tile)
            across = jnp.concatenate([tile, jnp.zeros((64, HD), F32)], axis=0).T
            both = jnp.where(lanes((KVH, HD)) < 64, across[:KVH], pltpu.roll(across[KVH:2 * KVH], 64, 1))
            for c in range(NY):
                ost[p, c] = both[2 * c:2 * c + 2]

        def query(i, k):
            return qslot[2 * p + i, (y - k // 2 + NY) % NY, (k % 2) * 32:(k % 2 + 1) * 32, :]

        attend(moved, taken(2 * p), taken(2 * p + 1), query, finish)

    for p in (0, 1):
        whole(qslot.at[2 * p:min(2 * p + 2, NR - 1)], QX, slot_rs.at[p]).wait_recv()
        taken_pair(p)
        for o in range(2 * p + 1, min(2 * p + 3, NR)):
            for yo in range(NY):
                push(obs.at[o - 1, (y + yo) % NY], rbs.at[o - 1, yo], OX, near(o, yo))
                push(ost.at[p, (y + yo) % NY], rst.at[o - 1, yo], OS, near(o, yo))

    whole(qyz.at[1:NZ], QYZ).wait_recv()
    for c in range(NT):
        four = qyz[(z - c % NZ + NZ) % NZ, (y - c // NZ + NY) % NY].astype(F32)
        for r in range(ROWS):
            macc[r, c * 8:(c + 1) * 8, :] = four[r * 8:(r + 1) * 8]
    for r in range(ROWS):
        qown[r] = macc[r].astype(BF16)
    lax.fori_loop(0, ROWS // 2, own_pair, 0)
    for c in range(NZ):
        obo[c, OWN - 16:OWN, :] = sto[c].astype(BF16)
    for o in zorder:
        push(obo.at[(z + o) % NZ], rbo.at[o - 1], OZY, near(zo=o))

    for p in (2, 3):
        whole(qslot.at[2 * p:min(2 * p + 2, NR - 1)], QX, slot_rs.at[p]).wait_recv()
        taken_pair(p)
        for o in range(2 * p + 1, min(2 * p + 3, NR)):
            for yo in range(NY):
                push(obs.at[o - 1, (y + yo) % NY], rbs.at[o - 1, yo], OX, near(o, yo))
                push(ost.at[p, (y + yo) % NY], rst.at[o - 1, yo], OS, near(o, yo))

    whole(rst, OS).wait_recv()
    index = [jnp.minimum((me - plan[e, 0, me] + 2 * NR - 1) % NR, NR - 2) for e in range(STEAL_IN)]
    row8 = lax.broadcasted_iota(jnp.int32, (8, HD), 0) // 2
    second = jnp.zeros((8, HD), jnp.int32)
    for e in range(STEAL_IN):
        second = jnp.where(row8 == e, index[e] % 2, second)
    tops = []
    for i in range(NY):
        tile = jnp.concatenate([rst[index[e], i] for e in range(STEAL_IN)] + [jnp.zeros((2, HD), F32)], axis=0)
        tops.append(jnp.where(second == 1, pltpu.roll(tile, 96, 1), tile))
    top = functools.reduce(jnp.maximum, tops)
    factors = [jnp.exp(one - top) for one in tops]
    total = sum(f * pltpu.roll(one, 64, 1) for f, one in zip(factors, tops))
    down = jnp.concatenate(factors + [top, total, jnp.zeros((HD - 48, HD), F32)], axis=0).T

    def down_column(i, e):
        first = i * 8 + 2 * e
        return jnp.concatenate([down[:32, first:first + 1], down[:32, first + 1:first + 2]], axis=0)

    whole(rbs, OX).wait_recv()
    marks = [jnp.zeros((64, HD), F32) for _ in range(2)]
    taken_acc = []
    for e in range(STEAL_IN):
        taken_acc.append(sum(down_column(i, e) * rbs[index[e], i].astype(F32) for i in range(NY)))
        marks[e % 2] = stamp(marks[e % 2], halves(down_column(NY, e)) + halves(down_column(NY + 1, e)), e // 2 * 4)
    for c in range(NZ):
        rows = slice(c * 8, (c + 1) * 8)
        mb[c, 0:32, :] = jnp.concatenate([acc[rows] for acc in taken_acc] + [jnp.zeros((8, HD), F32)], axis=0).astype(BF16)
        mb[c, 32:LAST, :] = jnp.concatenate([mark[rows] for mark in marks], axis=0).astype(BF16)
    for o in zorder:
        push(mb.at[(z + o) % NZ], zb.at[o - 1], OZ, near(zo=o))

    whole(rbo, OZY).wait_recv()
    acc, top, total = merged([obo[z]] + [rbo[i] for i in range(NZ - 1)], NY * 32)
    pieces = halves(top) + halves(total)
    lane16 = lanes((16, HD))
    for c in range(NY):
        mo[c, 0:32, :] = acc[c * 32:(c + 1) * 32].astype(BF16)
        tile = jnp.zeros((16, HD), F32)
        for p in range(2):
            for i, piece in enumerate(pieces):
                tile = jnp.where(lane16 == p * 4 + i, piece[c * 32 + p * 16:c * 32 + p * 16 + 16], tile)
        mo[c, 32:LAST, :] = tile.astype(BF16)
    for yo in range(1, NY):
        push(mo.at[(y + yo) % NY], yb.at[yo - 1], OY, near(yo=yo))

    whole(fz, FZ).wait_recv()
    for kind in range(2):
        acc = fsum[z // 4, kind]
        for o in range(1, NZ):
            acc = acc + fz[o - 1, kind]
        fresh[kind] = acc.astype(BF16).astype(F32)

    def new_rows(kind, s):
        return jnp.concatenate(
            [jnp.broadcast_to(fresh[kind, s * 8 + r:s * 8 + r + 1, :], (8, HD)) for r in range(8)], axis=0
        )

    late = lax.broadcasted_iota(jnp.int32, (64, 1), 0) % 8 >= 4
    query = qt[...]
    tail = [jnp.sum(query * new_rows(0, s), axis=1, keepdims=True) * INV for s in range(2)]
    tail[1] = jnp.where(late, tail[1], MASKED)
    tail_top = jnp.maximum(tail[0], tail[1])

    whole(yb, OY).wait_recv()
    own = merged([mo[y]] + [yb[i] for i in range(NY - 1)], 32)
    whole(zb, OZ).wait_recv()
    others = merged([mb[z]] + [zb[i] for i in range(NZ - 1)], 32)
    acc, top, total = [jnp.concatenate(both, axis=0) for both in zip(own, others)]
    peak = jnp.maximum(top, tail_top)
    factor = jnp.exp(top - peak)
    first = jnp.exp(tail[0] - peak)
    second = jnp.where(late, jnp.exp(tail[1] - peak), 0.0)
    total = total * factor + first + second
    acc = acc * factor
    acc = acc + first.astype(BF16).astype(F32) * new_rows(1, 0)
    acc = acc + second.astype(BF16).astype(F32) * new_rows(1, 1)
    fin[...] = acc / total
    for s in range(2):
        for j in range(4):
            out_ref[:, s, j * HD:(j + 1) * HD] = fin[pl.ds(s * 4 + j, ROWS_ALL, stride=8), :].astype(BF16)

    whole(qz.at[1:NZ], QZ).wait_send()
    whole(qyz.at[0, 1:NY], QY).wait_send()
    whole(qyz.at[1:NZ], QYZ).wait_send()
    whole(frecv, FY).wait_send()
    whole(qslot.at[0:NR - 1], QX).wait_send()
    whole(fz, FZ).wait_send()
    whole(rbo, OZY).wait_send()
    whole(rbs, OX).wait_send()
    whole(rst, OS).wait_send()
    whole(yb, OY).wait_send()
    whole(zb, OZ).wait_send()


def on_device(kv_pool, page_table, lengths, steal_plan, hidden_rows, kv_weight, queries):
    hbm = pl.BlockSpec(memory_space=pltpu.HBM)
    width = 2 * KVH * HD

    def half(*shape):
        return pltpu.VMEM((*shape, HD), BF16)

    def full(*shape):
        return pltpu.VMEM((*shape, HD), F32)

    out = pl.pallas_call(
        kernel,
        out_shape=pltpu.VMEM((ROWS_ALL, 2, 512), BF16),
        in_specs=[hbm] * 7,
        out_specs=pl.BlockSpec(memory_space=pltpu.VMEM),
        scratch_shapes=[
            pltpu.SMEM((ROWS, PPD), jnp.int32),
            pltpu.SMEM((ROWS, NR), jnp.int32),
            pltpu.SMEM((STEAL_IN, 2, NR), jnp.int32),
            pltpu.VMEM((ROWS_ALL, 2, 512), BF16),
            pltpu.VMEM((ROWS_ALL, 2, 512), BF16),
            pltpu.VMEM((SLOTS, PAGE, width), BF16),
            pltpu.VMEM((SLOTS, PAGE, width), BF16),
            pltpu.VMEM((512, width), BF16),
            full(64), half(NZ, 32), half(NZ, NY, 32), half(ROWS, 256), half(NR - 1, 64), half(NR, NY, 64),
            full(NY, 2, 2, 16), full(NY - 1, 2, 2, 16), full(2, 2, 16), full(NZ - 1, 2, 16), full(2, 16),
            half(NZ, OWN), half(NZ - 1, OWN), half(NR, NY, 64), half(NR - 1, NY, 64), full(NR // 2, NY, 2), full(NR - 1, NY, 2),
            full(NZ, 16), full(ROWS, 256), half(NY, LAST), half(NY - 1, LAST), half(NZ, LAST), half(NZ - 1, LAST),
            full(64),
            pltpu.SemaphoreType.DMA((7,)),
            pltpu.SemaphoreType.DMA((11,)),
            pltpu.SemaphoreType.DMA((11,)),
            pltpu.SemaphoreType.DMA((NR // 2,)),
        ],
        compiler_params=pltpu.CompilerParams(
            collective_id=0, has_side_effects=True, vmem_limit_bytes=63 * 2**20
        ),
    )(
        page_table[0], lengths.T, steal_plan.transpose(1, 2, 0), queries[0].transpose(1, 0, 2),
        hidden_rows[0].transpose(1, 0, 2), kv_pool[0], kv_weight,
    )
    return out.transpose(1, 0, 2)[None]


def solution(mesh):
    return jax.shard_map(
        on_device,
        mesh=mesh,
        in_specs=(
            P("replica", "tensor", None, None),
            P("replica", None, "tensor"),
            P(),
            P(),
            P("replica", None, None, "tensor"),
            P("tensor", None),
            P("replica", None, None, "tensor"),
        ),
        out_specs=P("replica", None, None, "tensor"),
        check_vma=False,
    )
```

```python
import functools
import math

import jax
import jax.numpy as jnp
from jax import lax
from jax.experimental import pallas as pl
from jax.experimental.pallas import tpu as pltpu
from jax.sharding import PartitionSpec as P

KVH = 8
HD = 128
PAGE = 32
PPD = 4
STEAL_IN = 3
ROWS = 4
ROWS_ALL = 7
SLOTS = 16
NR = 8
NY = 4
NZ = 8
NT = NY * NZ
MASKED = -1e30
MESH = pl.DeviceIdType.MESH
F32 = jnp.float32
BF16 = jnp.bfloat16
INV = 1.0 / math.sqrt(HD)
OWN = NY * ROWS * 8 + 16
LAST = 32 + 16


def lanes(shape):
    return lax.broadcasted_iota(jnp.int32, shape, len(shape) - 1)


def halves(x):
    high = x.astype(BF16).astype(F32)
    return high, (x - high).astype(BF16).astype(F32)


def stat_factors(tiles):
    tops = [tile + pltpu.roll(tile, 127, 1) for tile in tiles]
    totals = [pltpu.roll(one, 126, 1) for one in tops]
    top = functools.reduce(jnp.maximum, tops)
    factors = [jnp.exp(one - top) for one in tops]
    total = sum(f * l for f, l in zip(factors, totals))
    return top, total, factors


def column(x, groups):
    return jnp.concatenate([x[:, 4 * g:4 * g + 1] for g in range(groups)], axis=0)


def merged(held, rows):
    groups = rows // 16
    top, total, factors = stat_factors([part[rows:rows + 16].astype(F32) for part in held])
    acc = sum(column(f, groups) * part[:rows].astype(F32) for f, part in zip(factors, held))
    return acc, column(top, groups), column(total, groups)


def kernel(
    table_hbm, lengths_hbm, plan_hbm, q_hbm, h_hbm, pool_hbm, w_hbm, out_ref,
    table, lengths, plan, q_ref, h_ref, pool, moved, w, qt, qz, qyz, qown, qsend, qslot,
    fsend, frecv, fsum, fz, fresh, obo, rbo, obs, rbs, ost, rst, sto, macc, mo, yb, mb, zb, fin,
    lsem, ss, rs, slot_rs,
):
    me = lax.axis_index("replica")
    t = lax.axis_index("tensor")
    y, z = t // NZ, t % NZ

    def near(o=0, yo=0, zo=0):
        return ((me + o) % NR, ((y + yo) % NY) * NZ + (z + zo) % NZ)

    zorder = (4, 3, 5, 2, 6, 1, 7)

    pairs = (
        (q_hbm, q_ref), (plan_hbm, plan), (h_hbm, h_ref), (w_hbm, w),
        (pool_hbm, pool), (table_hbm, table), (lengths_hbm, lengths),
    )
    copies = [pltpu.make_async_copy(src, dst, lsem.at[i]) for i, (src, dst) in enumerate(pairs)]
    q_copy, plan_copy, h_copy, w_copy, pool_copy, table_copy, lengths_copy = copies
    for copy in copies:
        copy.start()

    barrier = pltpu.get_barrier_semaphore()
    peers = [near(zo=o) for o in zorder] + [near(yo=o) for o in range(1, NY)]
    peers += [near(o, yo) for o in range(1, NR) for yo in range(NY)]
    for peer in peers:
        pl.semaphore_signal(barrier, inc=1, device_id=peer, device_id_type=MESH)

    q_copy.wait()
    for s in range(2):
        for j in range(4):
            qt[pl.ds(s * 4 + j, ROWS_ALL, stride=8), :] = q_ref[:, s, j * HD:(j + 1) * HD].astype(F32)
    qt[56:64] = jnp.zeros((8, HD), F32)
    qz[0] = qt[32:64].astype(BF16)
    qyz[0, 0] = qt[0:32].astype(BF16)
    qslot[NR - 1] = jnp.zeros((NY, 64, HD), BF16)
    sto[...] = jnp.zeros_like(sto)

    def push(src, dst, stage, peer, recv=None):
        pltpu.make_async_remote_copy(
            src_ref=src, dst_ref=dst, send_sem=ss.at[stage], recv_sem=rs.at[stage] if recv is None else recv,
            device_id=peer, device_id_type=MESH,
        ).start()

    def whole(ref, stage, recv=None):
        return pltpu.make_async_remote_copy(
            src_ref=ref, dst_ref=ref, send_sem=ss.at[stage], recv_sem=rs.at[stage] if recv is None else recv,
            device_id=near(1), device_id_type=MESH,
        )

    QZ, QY, QYZ, QX, FY, FZ, OZY, OY, OX, OS, OZ = range(11)

    pl.semaphore_wait(barrier, len(peers))

    for o in zorder:
        push(qz.at[0], qz.at[o], QZ, near(zo=o))
    for yo in range(1, NY):
        push(qyz.at[0, 0], qyz.at[0, yo], QY, near(yo=yo))

    w_copy.wait()
    h_copy.wait()
    gap = jnp.zeros((1, 512), F32)
    hidden = jnp.concatenate([h_ref[:, 0].astype(F32), gap, h_ref[:, 1].astype(F32), gap], axis=0).astype(BF16)
    for kind in range(2):
        for k in range(0, KVH, 2):
            first = (kind * KVH + k) * HD
            part = jnp.dot(hidden, w[:, first:first + 2 * HD], preferred_element_type=F32)
            fsend[k // 2, 0, kind] = part[:, :HD]
            fsend[k // 2, 1, kind] = part[:, HD:]
    for yo in range(1, NY):
        push(fsend.at[(y + yo) % NY], frecv.at[yo - 1], FY, near(yo=yo))

    plan_copy.wait()
    whole(qz.at[1:NZ], QZ).wait_recv()
    chunks = [qz[(z - c + NZ) % NZ].astype(F32) for c in range(NZ)]

    def by_row(r):
        return jnp.concatenate([chunk[r * 8:(r + 1) * 8] for chunk in chunks], axis=0)

    leaving = [by_row(e) for e in range(STEAL_IN)]
    for o in range(1, NR):
        source = (me - o + NR) % NR
        chosen = jnp.zeros((64, HD), F32)
        for e in range(STEAL_IN):
            chosen = chosen + jnp.where(plan[e, 0, me] == source, leaving[e], 0.0)
        qsend[o - 1] = chosen.astype(BF16)
        for yo in range(NY):
            push(qsend.at[o - 1], qslot.at[o - 1, yo], QX, near(-o + NR, yo), slot_rs.at[(o - 1) // 2])

    whole(qyz.at[0, 1:NY], QY).wait_recv()
    for o in zorder:
        push(qyz.at[0], qyz.at[o], QYZ, near(zo=o))
    whole(frecv, FY).wait_recv()
    for c in range(2):
        for kind in range(2):
            fsum[c, kind] = fsend[y, c, kind] + frecv[0, c, kind] + frecv[1, c, kind] + frecv[2, c, kind]
    for o in zorder:
        push(fsum.at[((z + o) % NZ) // 4], fz.at[o - 1], FZ, near(zo=o))

    row_id = lax.broadcasted_iota(jnp.int32, (HD, HD), 0)
    both = jnp.bitwise_and(row_id, lanes((HD, HD)))
    parity = jnp.zeros((HD, HD), jnp.int32)
    for bit in range(7):
        parity = parity + jnp.bitwise_and(jnp.right_shift(both, bit), 1)
    signs = (1.0 - 2.0 * jnp.bitwise_and(parity, 1).astype(F32)).astype(BF16)

    pool_copy.wait()
    table_copy.wait()
    lengths_copy.wait()

    def round_trip(slot, carry):
        page = pool[slot]
        rows = jnp.concatenate([page[:, i * HD:(i + 1) * HD] for i in range(2 * KVH)], axis=0)
        turned = jnp.dot(rows, signs, preferred_element_type=F32) * INV
        scales = (jnp.max(jnp.abs(turned), axis=1, keepdims=True) + 1e-06).astype(BF16).astype(F32)
        packed = (turned * (1.0 / scales)).astype(BF16)
        back = (jnp.dot(packed, signs, preferred_element_type=F32) * (scales * INV)).astype(BF16)
        for i in range(2 * KVH):
            moved[slot, :, i * HD:(i + 1) * HD] = back[i * PAGE:(i + 1) * PAGE]
        return carry

    lax.fori_loop(0, SLOTS, round_trip, 0, unroll=4)

    lane64 = lanes((64, HD))
    row64 = lax.broadcasted_iota(jnp.int32, (64, HD), 0)
    upper = row64 < 32
    place = ((lane64 // PAGE) * NT + t) * PAGE + lane64 % PAGE
    blank = jnp.zeros((32, HD), BF16)

    def attend(pages, a, b, query, finish):
        (slots_a, span_a), (slots_b, span_b) = a, b
        valid = place < jnp.where(upper, span_a, span_b)

        def tokens(slots, first):
            return jnp.concatenate([pages[slot, :, first:first + HD] for slot in slots], axis=0)

        def spread(first, second):
            return jnp.concatenate(
                [jnp.concatenate([first, blank], axis=1), jnp.concatenate([blank, second], axis=1)], axis=0
            )

        scores, tops, lights, totals, mixed = [], [], [], [], []
        for k in range(KVH):
            wide = spread(query(0, k), query(1, k))
            keys = jnp.concatenate([tokens(slots_a, k * HD), tokens(slots_b, k * HD)], axis=1)
            scores.append(lax.dot_general(wide, keys, (((1,), (1,)), ((), ())), preferred_element_type=F32))
        for k in range(KVH):
            scores[k] = jnp.where(valid, scores[k] * INV, MASKED)
            tops.append(halves(jnp.max(scores[k], axis=1, keepdims=True)))
        for k in range(KVH):
            weights = jnp.where(valid, jnp.exp(scores[k] - (tops[k][0] + tops[k][1])), 0.0)
            totals.append(halves(jnp.sum(weights, axis=1, keepdims=True)))
            lights.append(weights.astype(BF16))
        for k in range(KVH):
            wide = spread(lights[k][:32], lights[k][32:])
            values = jnp.concatenate(
                [tokens(slots_a, (KVH + k) * HD), tokens(slots_b, (KVH + k) * HD)], axis=0
            )
            mixed.append(jnp.dot(wide, values, preferred_element_type=F32))
        finish(mixed, [top + total for top, total in zip(tops, totals)])

    def stamp(tile, pieces, first):
        for i, piece in enumerate(pieces):
            tile = jnp.where(lane64 == first + i, piece, tile)
        return tile

    def pages_of(request):
        return [table[request, j] for j in range(PPD)], lengths[request, me]

    def own_pair(p, carry):
        def finish(mixed, pieces):
            at = pl.multiple_of(p * 16, 16)
            for k in range(KVH):
                for j in range(4):
                    tile = jnp.concatenate([mixed[k][j * 8:j * 8 + 8], mixed[k][32 + j * 8:40 + j * 8]], axis=0)
                    obo[k % 2 * 4 + j, pl.ds(k // 2 * 32 + at, 16), :] = tile.astype(BF16)
            for half in range(2):
                tile = jnp.zeros((64, HD), F32)
                for k in range(half, KVH, 2):
                    tile = stamp(tile, pieces[k], (k // 2 * 2 + p) * 4)
                for j in range(4):
                    both = jnp.concatenate([tile[j * 8:j * 8 + 8], tile[32 + j * 8:40 + j * 8]], axis=0)
                    sto[half * 4 + j] = sto[half * 4 + j] + both

        def query(i, k):
            return qown[2 * p + i, k * 32:(k + 1) * 32, :]

        attend(pool, pages_of(2 * p), pages_of(2 * p + 1), query, finish)
        return carry

    def taken(o):
        taker = (me + o + 1) % NR
        request = jnp.int32(0)
        for e in range(STEAL_IN):
            request = request + jnp.where(plan[e, 0, taker] == me, plan[e, 1, taker], 0)
        return pages_of(request)

    def taken_pair(p):
        def finish(mixed, pieces):
            for k in range(KVH):
                for i in range(2):
                    obs[2 * p + i, k // 2, (k % 2) * 32:(k % 2 + 1) * 32, :] = mixed[k][i * 32:i * 32 + 32].astype(BF16)
            tile = jnp.zeros((64, HD), F32)
            for k in range(KVH):
                tile = jnp.where(lane64 == k, pieces[k][0] + pieces[k][1], tile)
                tile = jnp.where(lane64 == KVH + k, pieces[k][2] + pieces[k][3], tile)
            across = jnp.concatenate([tile, jnp.zeros((64, HD), F32)], axis=0).T
            both = jnp.where(lanes((KVH, HD)) < 64, across[:KVH], pltpu.roll(across[KVH:2 * KVH], 64, 1))
            for c in range(NY):
                ost[p, c] = both[2 * c:2 * c + 2]

        def query(i, k):
            return qslot[2 * p + i, (y - k // 2 + NY) % NY, (k % 2) * 32:(k % 2 + 1) * 32, :]

        attend(moved, taken(2 * p), taken(2 * p + 1), query, finish)

    for p in (0, 1):
        whole(qslot.at[2 * p:min(2 * p + 2, NR - 1)], QX, slot_rs.at[p]).wait_recv()
        taken_pair(p)
        for o in range(2 * p + 1, min(2 * p + 3, NR)):
            for yo in range(NY):
                push(obs.at[o - 1, (y + yo) % NY], rbs.at[o - 1, yo], OX, near(o, yo))
                push(ost.at[p, (y + yo) % NY], rst.at[o - 1, yo], OS, near(o, yo))

    whole(qyz.at[1:NZ], QYZ).wait_recv()
    for c in range(NT):
        four = qyz[(z - c % NZ + NZ) % NZ, (y - c // NZ + NY) % NY].astype(F32)
        for r in range(ROWS):
            macc[r, c * 8:(c + 1) * 8, :] = four[r * 8:(r + 1) * 8]
    for r in range(ROWS):
        qown[r] = macc[r].astype(BF16)
    lax.fori_loop(0, ROWS // 2, own_pair, 0)
    for c in range(NZ):
        obo[c, OWN - 16:OWN, :] = sto[c].astype(BF16)
    for o in zorder:
        push(obo.at[(z + o) % NZ], rbo.at[o - 1], OZY, near(zo=o))

    for p in (2, 3):
        whole(qslot.at[2 * p:min(2 * p + 2, NR - 1)], QX, slot_rs.at[p]).wait_recv()
        taken_pair(p)
        for o in range(2 * p + 1, min(2 * p + 3, NR)):
            for yo in range(NY):
                push(obs.at[o - 1, (y + yo) % NY], rbs.at[o - 1, yo], OX, near(o, yo))
                push(ost.at[p, (y + yo) % NY], rst.at[o - 1, yo], OS, near(o, yo))

    whole(rst, OS).wait_recv()
    index = [jnp.minimum((me - plan[e, 0, me] + 2 * NR - 1) % NR, NR - 2) for e in range(STEAL_IN)]
    row8 = lax.broadcasted_iota(jnp.int32, (8, HD), 0) // 2
    second = jnp.zeros((8, HD), jnp.int32)
    for e in range(STEAL_IN):
        second = jnp.where(row8 == e, index[e] % 2, second)
    tops = []
    for i in range(NY):
        tile = jnp.concatenate([rst[index[e], i] for e in range(STEAL_IN)] + [jnp.zeros((2, HD), F32)], axis=0)
        tops.append(jnp.where(second == 1, pltpu.roll(tile, 96, 1), tile))
    top = functools.reduce(jnp.maximum, tops)
    factors = [jnp.exp(one - top) for one in tops]
    total = sum(f * pltpu.roll(one, 64, 1) for f, one in zip(factors, tops))
    down = jnp.concatenate(factors + [top, total, jnp.zeros((HD - 48, HD), F32)], axis=0).T

    def down_column(i, e):
        first = i * 8 + 2 * e
        return jnp.concatenate([down[:32, first:first + 1], down[:32, first + 1:first + 2]], axis=0)

    whole(rbs, OX).wait_recv()
    mark = jnp.zeros((64, HD), F32)
    taken_acc = []
    for e in range(STEAL_IN):
        taken_acc.append(sum(down_column(i, e) * rbs[index[e], i].astype(F32) for i in range(NY)))
        mark = stamp(mark, halves(down_column(NY, e)) + halves(down_column(NY + 1, e)), e * 4)
    for c in range(NZ):
        rows = slice(c * 8, (c + 1) * 8)
        mb[c] = jnp.concatenate([acc[rows] for acc in taken_acc] + [mark[rows]], axis=0).astype(BF16)
    for o in zorder:
        push(mb.at[(z + o) % NZ], zb.at[o - 1], OZ, near(zo=o))

    whole(rbo, OZY).wait_recv()
    acc, top, total = merged([obo[z]] + [rbo[i] for i in range(NZ - 1)], NY * 32)
    pieces = halves(top) + halves(total)
    lane16 = lanes((16, HD))
    for c in range(NY):
        mo[c, 0:32, :] = acc[c * 32:(c + 1) * 32].astype(BF16)
        tile = jnp.zeros((16, HD), F32)
        for p in range(2):
            for i, piece in enumerate(pieces):
                tile = jnp.where(lane16 == p * 4 + i, piece[c * 32 + p * 16:c * 32 + p * 16 + 16], tile)
        mo[c, 32:LAST, :] = tile.astype(BF16)
    for yo in range(1, NY):
        push(mo.at[(y + yo) % NY], yb.at[yo - 1], OY, near(yo=yo))

    whole(fz, FZ).wait_recv()
    for kind in range(2):
        acc = fsum[z // 4, kind]
        for o in range(1, NZ):
            acc = acc + fz[o - 1, kind]
        fresh[kind] = acc.astype(BF16).astype(F32)

    def new_rows(kind, s):
        return jnp.concatenate(
            [jnp.broadcast_to(fresh[kind, s * 8 + r:s * 8 + r + 1, :], (8, HD)) for r in range(8)], axis=0
        )

    late = lax.broadcasted_iota(jnp.int32, (64, 1), 0) % 8 >= 4
    query = qt[...]
    tail = [jnp.sum(query * new_rows(0, s), axis=1, keepdims=True) * INV for s in range(2)]
    tail[1] = jnp.where(late, tail[1], MASKED)
    tail_top = jnp.maximum(tail[0], tail[1])

    whole(yb, OY).wait_recv()
    own = merged([mo[y]] + [yb[i] for i in range(NY - 1)], 32)
    whole(zb, OZ).wait_recv()
    held = [mb[z].astype(F32)] + [zb[i].astype(F32) for i in range(NZ - 1)]
    top, total, factors = stat_factors([part[24:32] for part in held])
    none = jnp.zeros((8, 1), F32)

    def by_entry(x):
        return jnp.concatenate([x[:, 4 * e:4 * e + 1] for e in range(STEAL_IN)] + [none], axis=0)

    others = sum(by_entry(f) * part for f, part in zip(factors, held)), by_entry(top), by_entry(total)
    acc, top, total = [jnp.concatenate(both, axis=0) for both in zip(own, others)]
    peak = jnp.maximum(top, tail_top)
    factor = jnp.exp(top - peak)
    first = jnp.exp(tail[0] - peak)
    second = jnp.where(late, jnp.exp(tail[1] - peak), 0.0)
    total = total * factor + first + second
    acc = acc * factor
    acc = acc + first.astype(BF16).astype(F32) * new_rows(1, 0)
    acc = acc + second.astype(BF16).astype(F32) * new_rows(1, 1)
    fin[...] = acc / total
    for s in range(2):
        for j in range(4):
            out_ref[:, s, j * HD:(j + 1) * HD] = fin[pl.ds(s * 4 + j, ROWS_ALL, stride=8), :].astype(BF16)

    whole(qz.at[1:NZ], QZ).wait_send()
    whole(qyz.at[0, 1:NY], QY).wait_send()
    whole(qyz.at[1:NZ], QYZ).wait_send()
    whole(frecv, FY).wait_send()
    whole(qslot.at[0:NR - 1], QX).wait_send()
    whole(fz, FZ).wait_send()
    whole(rbo, OZY).wait_send()
    whole(rbs, OX).wait_send()
    whole(rst, OS).wait_send()
    whole(yb, OY).wait_send()
    whole(zb, OZ).wait_send()


def on_device(kv_pool, page_table, lengths, steal_plan, hidden_rows, kv_weight, queries):
    hbm = pl.BlockSpec(memory_space=pltpu.HBM)
    width = 2 * KVH * HD

    def half(*shape):
        return pltpu.VMEM((*shape, HD), BF16)

    def full(*shape):
        return pltpu.VMEM((*shape, HD), F32)

    out = pl.pallas_call(
        kernel,
        out_shape=pltpu.VMEM((ROWS_ALL, 2, 512), BF16),
        in_specs=[hbm] * 7,
        out_specs=pl.BlockSpec(memory_space=pltpu.VMEM),
        scratch_shapes=[
            pltpu.SMEM((ROWS, PPD), jnp.int32),
            pltpu.SMEM((ROWS, NR), jnp.int32),
            pltpu.SMEM((STEAL_IN, 2, NR), jnp.int32),
            pltpu.VMEM((ROWS_ALL, 2, 512), BF16),
            pltpu.VMEM((ROWS_ALL, 2, 512), BF16),
            pltpu.VMEM((SLOTS, PAGE, width), BF16),
            pltpu.VMEM((SLOTS, PAGE, width), BF16),
            pltpu.VMEM((512, width), BF16),
            full(64), half(NZ, 32), half(NZ, NY, 32), half(ROWS, 256), half(NR - 1, 64), half(NR, NY, 64),
            full(NY, 2, 2, 16), full(NY - 1, 2, 2, 16), full(2, 2, 16), full(NZ - 1, 2, 16), full(2, 16),
            half(NZ, OWN), half(NZ - 1, OWN), half(NR, NY, 64), half(NR - 1, NY, 64), full(NR // 2, NY, 2), full(NR - 1, NY, 2),
            full(NZ, 16), full(ROWS, 256), half(NY, LAST), half(NY - 1, LAST), half(NZ, 32), half(NZ - 1, 32),
            full(64),
            pltpu.SemaphoreType.DMA((7,)),
            pltpu.SemaphoreType.DMA((11,)),
            pltpu.SemaphoreType.DMA((11,)),
            pltpu.SemaphoreType.DMA((NR // 2,)),
        ],
        compiler_params=pltpu.CompilerParams(
            collective_id=0, has_side_effects=True, vmem_limit_bytes=63 * 2**20
        ),
    )(
        page_table[0], lengths.T, steal_plan.transpose(1, 2, 0), queries[0].transpose(1, 0, 2),
        hidden_rows[0].transpose(1, 0, 2), kv_pool[0], kv_weight,
    )
    return out.transpose(1, 0, 2)[None]


def solution(mesh):
    return jax.shard_map(
        on_device,
        mesh=mesh,
        in_specs=(
            P("replica", "tensor", None, None),
            P("replica", None, "tensor"),
            P(),
            P(),
            P("replica", None, None, "tensor"),
            P("tensor", None),
            P("replica", None, None, "tensor"),
        ),
        out_specs=P("replica", None, None, "tensor"),
        check_vma=False,
    )
```
